256 devices in a mesh: gx: 32 (over z, x_hi, core), gy: 8 (over x_lo, y).
Axes of the slice: x: 4 (x_hi: 2, x_lo: 2; x = x_hi * 2 + x_lo), y: 4, z: 8, core: 2. Of those that a mesh axis runs over, the one named last changes fastest.
Arguments:
- e_adjoint: float32 [3, 512, 128, 256], P(None, 'gx', 'gy'), may hold values from -6 to 6
- h_adjoint: float32 [3, 512, 128, 256], P(None, 'gx', 'gy'), may hold values from -6 to 6
- sigma: float32 [3, 512, 128, 256], P(None, 'gx', 'gy'), may hold values from 0.1 to 3
- e_forward: bfloat16 [2, 3, 512, 128, 256], P(None, None, 'gx', 'gy'), may hold values from -6 to 6
- misfit: float32 [98304, 2, 256], P(('gx', 'gy')), may hold values from -6 to 6
- dest_tile: int32 [98304, 1], P(('gx', 'gy')), may hold values from 0 to 31; in each aligned block of 384 rows (0 to 383, 384 to 767, ...) at most 48 rows name the same one
- recv_cell: int32 [98304], P(('gx', 'gy')), may hold values from 0 to 65535
- time_weights: float32 [2, 256], replicated, may hold values from -0.375 to 0.375
Outputs:
- e_out: float32 [3, 512, 128, 256], P(None, 'gx', 'gy')
- h_out: float32 [3, 512, 128, 256], P(None, 'gx', 'gy')
- gradient: float32 [3, 512, 128, 256], P(None, 'gx', 'gy')
The draws below stay inside these ranges and needn't reach their ends.
Inputs may be any that keep to these rules, and one draw needn't show every extreme that they name: `dest_tile`: rows of one device name their receivers' tiles only in that device's own gy column; among the rows of one device at most 48 go to one tile, and in every draw some tile receives exactly 48 from some device.
All inputs are finite; a program needn't handle non-finite values.
Results may differ from the reference program's by a relative error of at most 0.0003.
Values sent between devices are 32-bit elements; how exact they have to be, the bound alone decides.
No kernel may reach another device: no remote copies, remote signals or barrier semaphores. Data moves between devices by JAX's collectives and lax.ppermute only.
A program may use at most 64 MiB of HBM per device.

```python
import math
import jax
import jax.numpy as jnp
import numpy as np
from jax import lax

CX = 16
CY = 16
NZ = 256
SAMPLES = 256
STEPS = 2
RD = 384
CAP = 48
NX = 512
NY = 128
ROWS = 98304
N_GX = 32
N_GY = 8


def with_ends(array, rng, smallest, top_value):
    longest = array.shape.index(max(array.shape))
    spots = []
    for shift in (0, 1):
        where = [jax.random.randint(jax.random.fold_in(rng, axis), (), 0, length) for axis, length in enumerate(array.shape)]
        where[longest] = (where[longest] + shift) % array.shape[longest]
        spots.append(tuple(where))
    return array.at[spots[0]].set(smallest).at[spots[1]].set(top_value)


def block_scale(stream_key, extent, split, smallest, largest):
    loudness, own = 1.0, jax.random.fold_in(stream_key, 6)
    for axis_at, shards_of in split:
        steps = jnp.exp(jax.random.uniform(jax.random.fold_in(own, axis_at), (shards_of,), jnp.float32, smallest / len(split), largest / len(split)))
        loudness = loudness * jnp.repeat(steps, extent[axis_at] // shards_of).reshape([-1 if axis == axis_at else 1 for axis in range(len(extent))])
    return loudness


def shared_out(own_key, own, number, rows, amount, top, most, slope):
    order = jax.random.permutation(own_key, amount)
    packed, usual = load_shares(amount, rows * top, most, slope, True), load_shares(amount, rows * top, most, slope, False)
    places = jnp.arange(amount)

    def named(tallies, turn):
        used = int((tallies > 0).sum())
        fixed = max(1, used // 4)
        moved = fixed + (places - fixed + turn * (used - fixed)) % max(1, amount - fixed)
        return jnp.zeros((amount,), jnp.int32).at[order[jnp.where(places < fixed, places, moved)]].set(jnp.asarray(tallies, jnp.int32))

    tallies = jnp.where(number % 4 == 0, named(packed, number // 4), named(usual, number - number // 4 - 1))
    mixed = jax.random.permutation(jax.random.fold_in(own, 3), amount)
    giver, taker = mixed[0:amount // 2 * 2:2], mixed[1:amount // 2 * 2:2]
    margin = jnp.minimum(tallies[giver] - 1, most - tallies[taker]) // 2
    margin = jnp.where((giver == order[0]) | (taker == order[0]) | (tallies[taker] == 0), 0, jnp.maximum(margin, 0))
    moved = jax.random.randint(jax.random.fold_in(own, 4), (amount // 2,), 0, 1 << 20) % (margin + 1)
    tallies = tallies.at[giver].add(-moved).at[taker].add(moved)
    items = jnp.searchsorted(jnp.cumsum(tallies), jnp.arange(rows * top), side="right").astype(jnp.int32)
    grid = items.reshape(top, rows).T
    grid = grid[jax.random.permutation(jax.random.fold_in(own, 1), rows)]
    turn = jax.random.randint(jax.random.fold_in(own, 2), (rows, 1), 0, top)
    return jnp.take_along_axis(grid, (jnp.arange(top)[None, :] + turn) % top, axis=1)


def load_shares(amount, total, limit, skew, full):
    weights = [(1 << 20) // math.isqrt(grade ** skew) + 1 for grade in range(1, amount + 1)]
    largest = limit if full else min(limit, max(-(-total // amount), total * weights[0] // sum(weights)))
    least = 1 if total - largest >= amount - 1 else 0
    holding, spare = [largest] + [least] * (amount - 1), total - largest - least * (amount - 1)
    while spare > 0:
        movable = [i for i in range(1, amount) if holding[i] < largest] or [i for i in range(1, amount) if holding[i] < limit]
        pool, remaining = sum([weights[i] for i in movable]), spare
        for i in movable:
            extra = min(limit - holding[i], max(1, remaining * weights[i] // pool), spare)
            holding[i] = holding[i] + extra
            spare = spare - extra
    return np.array(holding)


def noise(stream_key, extent, deviation, bound, pieces=(), kind=jnp.bfloat16):
    entries = jax.random.normal(stream_key, extent, jnp.float32) * deviation
    if len(pieces) > 0:
        entries = block_scale(stream_key, extent, pieces, -0.22, 0.18) * entries
    return jnp.clip(entries, min=-bound, max=bound).astype(kind)


def setup_inputs(seed: int = 0) -> dict:
    streams_of = jax.random.split(jax.random.key(seed), 9)
    e_adjoint = noise(streams_of[0], (3, NX, NY, NZ), 1.0, 6.0, ((1, 32), (2, 8)), jnp.float32)
    h_adjoint = noise(streams_of[1], (3, NX, NY, NZ), 1.0, 6.0, ((1, 32), (2, 8)), jnp.float32)
    sigma = jnp.clip(jnp.exp(math.log(3.0) - 3.4011974 * jax.random.uniform(streams_of[2], (3, NX, NY, NZ), jnp.float32) ** block_scale(streams_of[2], (3, NX, NY, NZ), ((1, 32), (2, 8)), -0.2, 0.2)), 0.1, 3.0)
    e_forward = noise(streams_of[3], (STEPS, 3, NX, NY, NZ), 1.0, 6.0, ((2, 32), (3, 8)))
    misfit = noise(streams_of[4], (ROWS, 2, SAMPLES), 1.0, 6.0, ((0, 256),), jnp.float32)
    dest_tile_keys = jax.random.split(jax.random.fold_in(streams_of[5], 1), ROWS // RD)
    dest_tile_turns = jax.random.permutation(jax.random.fold_in(streams_of[5], 3), ROWS // RD)
    dest_tile = jax.vmap(lambda own, number: shared_out(jax.random.fold_in(streams_of[5], 2), own, number, RD, N_GX, 1, CAP, 2))(dest_tile_keys, dest_tile_turns).reshape((ROWS, 1))
    recv_cell = with_ends(jax.random.randint(streams_of[6], (ROWS,), 0, CX * CY * NZ), jax.random.fold_in(streams_of[6], 1), 0, (CX * CY * NZ) - 1).astype(jnp.int32)
    time_weights = noise(streams_of[7], (STEPS, SAMPLES), SAMPLES ** -0.5, 0.375, (), jnp.float32)
    return {"e_adjoint": e_adjoint, "h_adjoint": h_adjoint, "sigma": sigma, "e_forward": e_forward, "misfit": misfit, "dest_tile": dest_tile, "recv_cell": recv_cell, "time_weights": time_weights}


def lower(field, axis):
    size = field.shape[axis]
    pads = [(0, 0)] * field.ndim
    pads[axis] = (1, 0)
    return lax.slice_in_dim(jnp.pad(field, pads), 0, size, axis=axis)


def upper(field, axis):
    size = field.shape[axis]
    pads = [(0, 0)] * field.ndim
    pads[axis] = (0, 1)
    return lax.slice_in_dim(jnp.pad(field, pads), 1, size + 1, axis=axis)


def curl_lower(hx, hy, hz):
    cx = (hz - lower(hz, 1)) - (hy - lower(hy, 2))
    cy = (hx - lower(hx, 2)) - (hz - lower(hz, 0))
    cz = (hy - lower(hy, 0)) - (hx - lower(hx, 1))
    return jnp.stack((cx, cy, cz))


def curl_upper(ex, ey, ez):
    cx = (upper(ez, 1) - ez) - (upper(ey, 2) - ey)
    cy = (upper(ex, 2) - ex) - (upper(ez, 0) - ez)
    cz = (upper(ey, 0) - ey) - (upper(ex, 1) - ex)
    return jnp.stack((cx, cy, cz))


def reference(e_adjoint, h_adjoint, sigma, e_forward, misfit, dest_tile, recv_cell, time_weights):
    amp = jnp.einsum("rcs,ks->kcr", misfit, time_weights, precision=lax.Precision.HIGHEST)
    rows = jnp.arange(misfit.shape[0], dtype=jnp.int32)
    column = (rows // RD) % N_GY
    local = recv_cell.astype(jnp.int32)
    xpos = dest_tile[:, 0].astype(jnp.int32) * CX + local // (CY * NZ)
    ypos = column * CY + (local // NZ) % CY
    zpos = local % NZ
    flat = (xpos * NY + ypos) * NZ + zpos
    source = jnp.zeros((STEPS, 2, NX * NY * NZ), jnp.float32).at[:, :, flat].add(amp)
    source = source.reshape(STEPS, 2, NX, NY, NZ)
    half = 0.5 * sigma
    ca = (1.0 - half) / (1.0 + half)
    cb = 0.5 / (1.0 + half)
    efield = e_adjoint
    hfield = h_adjoint
    gradient = jnp.zeros_like(e_adjoint)
    for step in range(STEPS):
        hfield = hfield - 0.5 * curl_upper(efield[0], efield[1], efield[2])
        drive = curl_lower(hfield[0], hfield[1], hfield[2])
        drive = drive.at[0:2].add(source[step])
        efield = ca * efield + cb * drive
        gradient = gradient + e_forward[step].astype(jnp.float32) * efield
    return efield, hfield, gradient
```

```python
import functools

import jax
import jax.numpy as jnp
from jax import lax
from jax.experimental import pallas as pl
from jax.experimental.pallas import tpu as pltpu
from jax.sharding import PartitionSpec as P

STEPS = 2
CAP = 48
NT = (((1,), (1,)), ((), ()))
VMEM = pl.BlockSpec(memory_space=pltpu.VMEM)
F32 = jnp.float32
BF16 = jnp.bfloat16


def shift(block, axis, distance):
    devices = range(lax.axis_size(axis))
    route = [(i - distance, i) for i in devices if i - distance in devices]
    return lax.ppermute(block, axis, route)


def call(kernel, args, outs, scratch=(), flops=0, name=None):
    outs = [jax.ShapeDtypeStruct(shape, dtype) for shape, dtype in outs]
    moved = sum(a.size * a.dtype.itemsize for a in list(args) + outs)
    return pl.pallas_call(
        kernel,
        out_shape=outs,
        in_specs=[VMEM] * len(args),
        out_specs=[VMEM] * len(outs),
        scratch_shapes=list(scratch),
        compiler_params=pltpu.CompilerParams(vmem_limit_bytes=40 * 1024 * 1024),
        cost_estimate=pl.CostEstimate(flops=flops, bytes_accessed=moved, transcendentals=0),
        name=name,
    )(*args)


def iota(shape, axis):
    return lax.broadcasted_iota(jnp.int32, shape, axis)


def pieces(value, count):
    parts = []
    for _ in range(count):
        part = value.astype(BF16)
        parts.append(part)
        value = value - part.astype(F32)
    return parts


def pack_kernel(tiles, rows, misfit_ref, dest_ref, cell_ref, weights_ref, out_ref):
    weights = weights_ref[...]
    amps = []
    for comp in range(2):
        total = None
        for half in range(2):
            block = misfit_ref[pl.ds(2 * half + comp, rows, stride=4), :]
            part = lax.dot_general(
                weights[:, half * 128:(half + 1) * 128], block, NT,
                precision=lax.Precision.HIGHEST, preferred_element_type=F32,
            )
            total = part if total is None else total + part
        amps.append(total)
    dest = dest_ref[...]
    named = (iota((tiles, rows), 0) == dest).astype(F32)
    earlier = (iota((rows, rows), 0) < iota((rows, rows), 1)).astype(F32).astype(BF16)
    before = jnp.dot(named.astype(BF16), earlier, preferred_element_type=F32)
    slot = jnp.sum(named * before, axis=0, keepdims=True).astype(jnp.int32)
    spread = (iota((128, rows), 0) == slot).astype(F32).astype(BF16)
    row = iota((8, rows), 0)
    fields = jnp.where(row == 4, cell_ref[...].astype(F32), 0.0)
    for k in range(STEPS):
        for comp in range(2):
            fields = jnp.where(row == 2 * k + comp, amps[comp][k:k + 1], fields)
    mask = iota((tiles, 8, rows), 0) == dest[None]
    total = None
    for part in pieces(fields, 3):
        left = jnp.where(mask, part.astype(F32)[None], 0.0).reshape(tiles * 8, rows).astype(BF16)
        product = lax.dot_general(left, spread, NT, preferred_element_type=F32)
        total = product if total is None else total + product
    out_ref[...] = total.reshape(tiles, 8, 128)


def z_up(a):
    return jnp.where(iota(a.shape, 1) == a.shape[1] - 1, 0.0, pltpu.roll(a, a.shape[1] - 1, 1))


def z_low(a):
    return jnp.where(iota(a.shape, 1) == 0, 0.0, pltpu.roll(a, 1, 1))


def y_up(a, row):
    return jnp.where(iota(a.shape, 0) == a.shape[0] - 1, row, pltpu.roll(a, a.shape[0] - 1, 0))


def y_low(a, row):
    return jnp.where(iota(a.shape, 0) == 0, row, pltpu.roll(a, 1, 0))


def magnetic_planes(e_ref, h_ref, fx_ref, fy_ref, h_out, sx_ref, sy_ref):
    nx = e_ref.shape[1]
    for x in range(nx):
        ex, ey, ez = e_ref[0, x], e_ref[1, x], e_ref[2, x]
        ey_x, ez_x = (e_ref[1, x + 1], e_ref[2, x + 1]) if x + 1 < nx else (fx_ref[0], fx_ref[1])
        ex_y = y_up(ex, fy_ref[0, x:x + 1])
        ez_y = y_up(ez, fy_ref[1, x:x + 1])
        hx = h_ref[0, x] - 0.5 * ((ez_y - ez) - (z_up(ey) - ey))
        hy = h_ref[1, x] - 0.5 * ((z_up(ex) - ex) - (ez_x - ez))
        hz = h_ref[2, x] - 0.5 * ((ey_x - ey) - (ex_y - ex))
        h_out[0, x] = hx
        h_out[1, x] = hy
        h_out[2, x] = hz
        last = hx.shape[0] - 1
        sy_ref[0, x:x + 1] = hx[last:]
        sy_ref[1, x:x + 1] = hz[last:]
        if x == nx - 1:
            sx_ref[0] = hy
            sx_ref[1] = hz


def drive_planes(x, h_ref, fx_ref, fy_ref):
    hx, hy, hz = h_ref[0, x], h_ref[1, x], h_ref[2, x]
    hy_x, hz_x = (h_ref[1, x - 1], h_ref[2, x - 1]) if x > 0 else (fx_ref[0], fx_ref[1])
    hx_y = y_low(hx, fy_ref[0, x:x + 1])
    hz_y = y_low(hz, fy_ref[1, x:x + 1])
    cx = (hz - hz_y) - (hy - z_low(hy))
    cy = (hx - z_low(hx)) - (hz - hz_x)
    cz = (hy - hy_x) - (hx - hx_y)
    return cx, cy, cz


def edge_kernel(e_ref, sx_ref, sy_ref):
    sx_ref[...] = e_ref[1:3, 0]
    for x in range(e_ref.shape[1]):
        sy_ref[0, x:x + 1] = e_ref[0, x, 0:1]
        sy_ref[1, x:x + 1] = e_ref[2, x, 0:1]


def coefficients(sigma):
    half = 0.5 * sigma
    under = 1.0 / (1.0 + half)
    return (1.0 - half) * under, 0.5 * under


def first_electric_kernel(e_ref, h_ref, sigma_ref, fx_ref, fy_ref, e_out):
    for x in range(e_ref.shape[1]):
        drive = drive_planes(x, h_ref, fx_ref, fy_ref)
        for c in range(3):
            ca, cb = coefficients(sigma_ref[c, x])
            e_out[c, x] = ca * e_ref[c, x] + cb * drive[c]


def scatter_kernel(tiles, recv_ref, e_ref, sigma_ref, e_out, late_ref, sx_ref, sy_ref, src_ref):
    nx, ny, nz = e_ref.shape[1], e_ref.shape[2], e_ref.shape[3]
    lane = iota((8, 128), 1)
    lists = []
    for pair in range(tiles // 2):
        lists.append(jnp.where(lane < 64, recv_ref[2 * pair], pltpu.roll(recv_ref[2 * pair + 1], 64, 1)))
    table = jnp.concatenate(lists, axis=1)
    depth = table.shape[1]
    cell = table[4:5].astype(jnp.int32)
    columns = nx * ny
    column_hot = (iota((columns, depth), 0) == cell // nz).astype(F32).astype(BF16)
    depth_hot = (iota((nz, depth), 0) == cell % nz).astype(F32).astype(BF16)
    high, low = pieces(table, 2)
    for field in range(4):
        product = None
        for part in (high, low):
            left = column_hot * part[field:field + 1]
            term = lax.dot_general(left, depth_hot, NT, preferred_element_type=F32)
            product = term if product is None else product + term
        if field < 2:
            src_ref[field] = product.reshape(nx, ny, nz)
        else:
            late_ref[field - 2] = product.reshape(nx, ny, nz)
    for x in range(nx):
        for c in range(3):
            e = e_ref[c, x]
            if c < 2:
                _, cb = coefficients(sigma_ref[c, x])
                e = e + cb * src_ref[c, x]
            e_out[c, x] = e
            if c != 1:
                sy_ref[c // 2, x:x + 1] = e[0:1]
            if x == 0 and c > 0:
                sx_ref[c - 1] = e


def last_kernel(e_ref, h_ref, sigma_ref, late_ref, fwd_ref, fx_ref, fy_ref, e_out, g_out):
    for x in range(e_ref.shape[1]):
        drive = drive_planes(x, h_ref, fx_ref, fy_ref)
        for c in range(3):
            ca, cb = coefficients(sigma_ref[c, x])
            before = e_ref[c, x]
            push = drive[c] + late_ref[c, x] if c < 2 else drive[c]
            after = ca * before + cb * push
            e_out[c, x] = after
            g_out[c, x] = fwd_ref[0, c, x].astype(F32) * before + fwd_ref[1, c, x].astype(F32) * after


def body(e_adjoint, h_adjoint, sigma, e_forward, misfit, dest_tile, recv_cell, time_weights):
    tiles = lax.axis_size("gx")
    rows = misfit.shape[0]
    grid = e_adjoint.shape
    nx, ny, nz = grid[1:]
    face_x, face_y = ((2, ny, nz), F32), ((2, nx, nz), F32)
    sx, sy = call(edge_kernel, [e_adjoint], [face_x, face_y], name="edges")
    upper_x, upper_y = shift(sx, "gx", -1), shift(sy, "gy", -1)
    lines = misfit.reshape(rows, 2, 2, 128).transpose(0, 2, 1, 3).reshape(rows * 4, 128)
    packed, = call(
        functools.partial(pack_kernel, tiles, rows),
        [lines, dest_tile.reshape(1, rows), recv_cell.reshape(1, rows), time_weights],
        [((tiles, 8, 128), F32)], flops=2 * 3 * 256 * rows * 128, name="pack",
    )
    received = lax.all_to_all(packed, "gx", split_axis=0, concat_axis=0, tiled=True)
    h1, sx, sy = call(magnetic_planes, [e_adjoint, h_adjoint, upper_x, upper_y], [(grid, F32), face_x, face_y], name="magnetic")
    lower_x, lower_y = shift(sx, "gx", 1), shift(sy, "gy", 1)
    e1, = call(first_electric_kernel, [e_adjoint, h1, sigma, lower_x, lower_y], [(grid, F32)], name="electric")
    e1, late, sx, sy = call(
        functools.partial(scatter_kernel, tiles), [received, e1, sigma],
        [(grid, F32), ((2,) + grid[1:], F32), face_x, face_y],
        scratch=[pltpu.VMEM((2,) + grid[1:], F32)], flops=2 * 8 * 256 * 2048 * 256, name="scatter",
    )
    upper_x, upper_y = shift(sx, "gx", -1), shift(sy, "gy", -1)
    h2, sx, sy = call(magnetic_planes, [e1, h1, upper_x, upper_y], [(grid, F32), face_x, face_y], name="magnetic")
    lower_x, lower_y = shift(sx, "gx", 1), shift(sy, "gy", 1)
    e2, gradient = call(last_kernel, [e1, h2, sigma, late, e_forward, lower_x, lower_y], [(grid, F32), (grid, F32)], name="final")
    return e2, h2, gradient


def solution(mesh):
    placed = (
        P(None, "gx", "gy", None),
        P(None, "gx", "gy", None),
        P(None, "gx", "gy", None),
        P(None, None, "gx", "gy", None),
        P(("gx", "gy"), None, None),
        P(("gx", "gy"), None),
        P(("gx", "gy")),
        P(),
    )
    return jax.shard_map(
        body,
        mesh=mesh,
        in_specs=placed,
        out_specs=(P(None, "gx", "gy", None), P(None, "gx", "gy", None), P(None, "gx", "gy", None)),
        check_vma=False,
    )
```

```python
import functools

import jax
import jax.numpy as jnp
from jax import lax
from jax.experimental import pallas as pl
from jax.experimental.pallas import tpu as pltpu
from jax.sharding import PartitionSpec as P

STEPS = 2
CAP = 48
NT = (((1,), (1,)), ((), ()))
VMEM = pl.BlockSpec(memory_space=pltpu.VMEM)
F32 = jnp.float32
BF16 = jnp.bfloat16


def shift(block, axis, distance):
    devices = range(lax.axis_size(axis))
    route = [(i - distance, i) for i in devices if i - distance in devices]
    return lax.ppermute(block, axis, route)


def call(kernel, args, outs, scratch=(), flops=0, name=None):
    outs = [jax.ShapeDtypeStruct(shape, dtype) for shape, dtype in outs]
    moved = sum(a.size * a.dtype.itemsize for a in list(args) + outs)
    return pl.pallas_call(
        kernel,
        out_shape=outs,
        in_specs=[VMEM] * len(args),
        out_specs=[VMEM] * len(outs),
        scratch_shapes=list(scratch),
        compiler_params=pltpu.CompilerParams(vmem_limit_bytes=40 * 1024 * 1024),
        cost_estimate=pl.CostEstimate(flops=flops, bytes_accessed=moved, transcendentals=0),
        name=name,
    )(*args)


def iota(shape, axis):
    return lax.broadcasted_iota(jnp.int32, shape, axis)


def hot(condition):
    return jnp.where(condition, 1.0, 0.0).astype(BF16)


def pieces(value):
    high = value.astype(BF16)
    return high, (value - high.astype(F32)).astype(BF16)


def turn(a, amount, axis):
    amount = amount % a.shape[axis]
    return a if amount == 0 else pltpu.roll(a, amount, axis)


def z_up(a):
    return jnp.where(iota(a.shape, 1) == a.shape[1] - 1, 0.0, turn(a, -1, 1))


def z_low(a):
    return jnp.where(iota(a.shape, 1) == 0, 0.0, turn(a, 1, 1))


def y_up(a):
    return turn(a, -1, 0)


def y_low(a):
    return turn(a, 1, 0)


def rows_kernel(rows, misfit_ref, dest_ref, cell_ref, weights_ref, e_ref, h_ref, s_ref, own_ref, up_ref, down_ref):
    weights = weights_ref[...]
    row = iota((8, rows), 0)
    fields = jnp.where(row == 4, cell_ref[...].astype(F32), 0.0)
    fields = jnp.where(row == 5, dest_ref[...].astype(F32), fields)
    for comp in range(2):
        total = None
        for half in range(2):
            block = misfit_ref[pl.ds(2 * half + comp, rows, stride=4), :]
            part = lax.dot_general(
                weights[:, half * 128:(half + 1) * 128], block, NT,
                precision=lax.Precision.HIGHEST, preferred_element_type=F32,
            )
            total = part if total is None else total + part
        for k in range(STEPS):
            fields = jnp.where(row == 2 * k + comp, total[k:k + 1], fields)
    own_ref[...] = fields
    nx = e_ref.shape[1]
    sub = iota((8, e_ref.shape[3]), 0)
    for x in range(nx):
        top = [[ref[c, x, 8:16] for c in range(3)] for ref in (e_ref, h_ref, s_ref)]
        low = [[ref[c, x, 0:8] for c in range(3)] for ref in (e_ref, h_ref, s_ref)]
        e, h, s = top
        three = [jnp.where(sub < 2, turn(f[0], 2, 0), jnp.where(sub < 4, turn(f[1], 4, 0), turn(f[2], 6, 0))) for f in (e, h)]
        up_ref[x] = jnp.where(sub < 6, three[0], jnp.where(sub == 6, turn(s[0], 7, 0), s[1]))
        up_ref[nx + x] = jnp.where(sub < 6, three[1], jnp.where(sub == 6, turn(s[2], 7, 0), 0.0))
        e, h, s = low
        three = jnp.where(sub < 2, e[0], jnp.where(sub < 4, turn(e[1], 2, 0), turn(e[2], 4, 0)))
        down_ref[x] = jnp.where(sub < 6, three, jnp.where(sub == 6, turn(s[0], 6, 0), turn(s[1], 7, 0)))
        three = jnp.where(sub == 0, h[0], jnp.where(sub == 1, turn(h[1], 1, 0), turn(h[2], 2, 0)))
        down_ref[nx + x] = jnp.where(sub < 3, three, jnp.where(sub == 3, turn(s[2], 3, 0), 0.0))
    for ref in (up_ref, down_ref):
        ref[2 * nx] = fields[:, 0:256]
        ref[2 * nx + 1] = jnp.concatenate([fields[:, 256:384], jnp.zeros((8, 128), F32)], axis=1)


def places(fields, tiles):
    rows = fields.shape[1]
    dest = fields[5:6].astype(jnp.int32)
    named = (iota((tiles, rows), 0) == dest).astype(F32)
    before = jnp.dot(named.astype(BF16), hot(iota((rows, rows), 0) < iota((rows, rows), 1)), preferred_element_type=F32)
    slot = jnp.sum(named * before, axis=0, keepdims=True).astype(jnp.int32)
    cell = fields[4:5].astype(jnp.int32)
    return dest, slot, cell // 4096, (cell // 256) % 16


def lay(fields, slot, offset, picks):
    tiles, rows = 32, fields.shape[1]
    row = iota((8, rows), 0)
    left = [jnp.zeros((8, rows), BF16).astype(F32)] * 2
    where = jnp.full((8, rows), -1, jnp.int32)
    for at, field, tile in picks:
        for number, part in enumerate(pieces(fields[field:field + 1])):
            left[number] = jnp.where(row == at, part.astype(F32), left[number])
        where = jnp.where(row == at, tile, where)
    mask = iota((tiles, 8, rows), 0) == where[None]
    spread = hot(iota((128, rows), 0) == slot + offset)
    total = None
    for part in left:
        block = jnp.where(mask, part[None], 0.0).reshape(tiles * 8, rows).astype(BF16)
        product = lax.dot_general(block, spread, NT, preferred_element_type=F32)
        total = product if total is None else total + product
    return total.reshape(tiles, 8, 128)


def own_kernel(tiles, fields_ref, out_ref):
    fields = fields_ref[...]
    dest, slot, x, _ = places(fields, tiles)
    after = jnp.where(x == 15, dest + 1, -1)
    ahead = jnp.where(x == 0, dest - 1, -1)
    out_ref[...] = lay(fields, slot, 0, [(i, i, dest) for i in range(5)]) + lay(
        fields, slot, 64, [(0, 0, after), (1, 1, after), (2, 4, after), (3, 1, ahead), (4, 4, ahead)]
    )


def message_kernel(tiles, nx, own_ref, up_ref, down_ref, out_ref):
    out_ref[:, 0:8] = own_ref[...]
    fields = jnp.concatenate([up_ref[2 * nx], up_ref[2 * nx + 1][:, 0:128]], axis=1)
    dest, slot, x, y = places(fields, tiles)
    here = jnp.where(y == 15, dest, -1)
    ahead = jnp.where((y == 15) & (x == 0), dest - 1, -1)
    block = lay(fields, slot, 0, [(0, 0, here), (1, 1, here), (2, 4, here)])
    block = block + lay(fields, slot, 64, [(0, 1, ahead), (1, 4, ahead)])
    fields = jnp.concatenate([down_ref[2 * nx], down_ref[2 * nx + 1][:, 0:128]], axis=1)
    dest, slot, x, y = places(fields, tiles)
    here = jnp.where(y == 0, dest, -1)
    after = jnp.where((y == 0) & (x == 15), dest + 1, -1)
    block = block + lay(fields, slot, 0, [(3, 0, here), (4, 4, here)])
    out_ref[:, 8:16] = block + lay(fields, slot, 64, [(2, 0, after), (3, 4, after)])


def halo_kernel(e_ref, h_ref, s_ref, up_ref, down_ref, halo_ref, right_ref, left_ref):
    nx = e_ref.shape[1]
    sub = iota((8, e_ref.shape[3]), 0)
    for x in range(nx):
        ua, ub, da, db = up_ref[x], up_ref[nx + x], down_ref[x], down_ref[nx + x]
        for c in range(3):
            halo_ref[c, x] = jnp.where(sub < 2, turn(da, -2 * c, 0), jnp.where(sub >= 6, turn(ua, 6 - 2 * c, 0), 0.0))
            halo_ref[3 + c, x] = jnp.where(sub < 1, turn(db, -c, 0), jnp.where(sub >= 6, turn(ub, 6 - 2 * c, 0), 0.0))
        pairs = ((turn(da, 2, 0), turn(ua, 1, 0)), (turn(da, 1, 0), ua), (turn(db, 5, 0), turn(ub, 1, 0)))
        for c in range(3):
            halo_ref[6 + c, x] = jnp.where(sub == 0, pairs[c][0], jnp.where(sub == 7, pairs[c][1], 0.0))

    def plane(field, c, x):
        ref = (e_ref, h_ref, s_ref)[field]
        return jnp.concatenate([ref[c, x], halo_ref[3 * field + c, x]], axis=0)

    for c in range(3):
        right_ref[2 * c] = plane(0, c, nx - 2)
        right_ref[2 * c + 1] = plane(0, c, nx - 1)
        right_ref[11 + c] = plane(2, c, nx - 1)
        left_ref[c] = plane(0, c, 0)
        left_ref[5 + c] = plane(1, c, 0)
        if c > 0:
            left_ref[2 + c] = plane(0, c, 1)
            left_ref[7 + c] = plane(2, c, 0)
    for at, c, x in ((6, 0, 1), (7, 1, 2), (8, 1, 1), (9, 2, 2), (10, 2, 1)):
        right_ref[at] = plane(1, c, nx - x)


def coefficients(sigma):
    half = 0.5 * sigma
    under = 1.0 / (1.0 + half)
    return (1.0 - half) * under, 0.5 * under


def curl_electric(e, after):
    ex, ey, ez = e
    cx = None if ey is None else (y_up(ez) - ez) - (z_up(ey) - ey)
    cy = (z_up(ex) - ex) - (after[2] - ez)
    cz = (after[1] - ey) - (y_up(ex) - ex)
    return cx, cy, cz


def curl_magnetic(h, before):
    hx, hy, hz = h
    cx = (hz - y_low(hz)) - (hy - z_low(hy))
    cy = (hx - z_low(hx)) - (hz - before[2])
    cz = (hy - before[1]) - (hx - y_low(hx))
    return cx, cy, cz


def first_kernel(e_ref, h_ref, s_ref, halo_ref, right_ref, left_ref, e_out, h_out, cb_out):
    nx = e_ref.shape[1]
    ring = iota((24, e_ref.shape[3]), 0)
    tables = (
        {(c, x): (right_ref, 2 * c + x + 2) for c in range(3) for x in (-2, -1)}
        | {(c, nx): (left_ref, c) for c in range(3)}
        | {(c, nx + 1): (left_ref, 2 + c) for c in (1, 2)},
        {(0, -1): (right_ref, 6), (1, -2): (right_ref, 7), (1, -1): (right_ref, 8), (2, -2): (right_ref, 9), (2, -1): (right_ref, 10)}
        | {(c, nx): (left_ref, 5 + c) for c in range(3)},
        {(c, -1): (right_ref, 11 + c) for c in range(3)} | {(c, nx): (left_ref, 7 + c) for c in (1, 2)},
    )

    def plane(field, c, x):
        if 0 <= x < nx:
            ref = (e_ref, h_ref, s_ref)[field]
            return jnp.concatenate([ref[c, x], halo_ref[3 * field + c, x]], axis=0)
        if (c, x) not in tables[field]:
            return None
        ref, at = tables[field][c, x]
        return ref[at]

    before = None
    for x in range(-2, nx + 1):
        e = [plane(0, c, x) for c in range(3)]
        curl = curl_electric(e, [plane(0, c, x + 1) for c in range(3)])
        h = []
        for c in range(3):
            value = plane(1, c, x)
            if value is not None:
                value = value - 0.5 * curl[c]
                if x > -2:
                    outside = plane(2, 1, x) <= 0.0
                    value = jnp.where(outside if x == -1 else outside & (ring == 23), 0.0, value)
            h.append(value)
            if -1 <= x < nx:
                h_out[c, x + 1] = value
        if x > -2:
            drive = curl_magnetic(h, before)
            for c in range(3):
                sigma = plane(2, c, x)
                if sigma is None:
                    e_out[c, x + 1] = jnp.zeros(e_out.shape[2:], F32)
                    cb_out[c, x + 1] = jnp.zeros(e_out.shape[2:], F32)
                    continue
                ca, cb = coefficients(sigma)
                inside = sigma > 0.0
                e_out[c, x + 1] = jnp.where(inside, ca * e[c] + cb * drive[c], 0.0)
                if c < 2:
                    cb_out[c, x + 1] = jnp.where(inside, cb, 0.0)
        before = h


def spots(cell, table, amps, position, places_, nz_hot):
    held = hot(iota((places_, table[0].shape[1]), 0) == position)
    left = jnp.concatenate([held * part[a:a + 1] for a in amps for part in table], axis=0)
    product = lax.dot_general(left, nz_hot, NT, preferred_element_type=F32)
    n = places_
    return [product[2 * i * n:(2 * i + 1) * n] + product[(2 * i + 1) * n:(2 * i + 2) * n] for i in range(len(amps))]


def final_kernel(tiles, recv_ref, e_ref, h_ref, cb_ref, s_ref, fwd_ref, e_out, h_out, g_out, src_ref, new_ref):
    nx, ny, nz = s_ref.shape[1], s_ref.shape[2], s_ref.shape[3]
    lane = iota((16, 128), 1)
    low, high = [], []
    for pair in range(tiles // 2):
        one, two = recv_ref[2 * pair], recv_ref[2 * pair + 1]
        low.append(jnp.where(lane < 64, one, turn(two, 64, 1)))
        high.append(jnp.where(lane < 64, turn(one, 64, 1), two))
    sums = {}

    def gather(name, whole, at, amps, kind):
        table = jnp.concatenate([part[8 * (at // 8):8 * (at // 8) + 8] for part in whole], axis=1)
        first = at % 8
        cell = table[first + len(amps):first + len(amps) + 1].astype(jnp.int32)
        depth_hot = hot(iota((nz, table.shape[1]), 0) == cell % nz)
        column = cell // nz
        position, count = {"cell": (column, nx * ny), "x": (column // ny, nx), "y": (column % ny, ny), "one": (column * 0, 16)}[kind]
        parts = pieces(table)
        if kind == "cell":
            held = hot(iota((count, table.shape[1]), 0) == position)
            for i in range(len(amps)):
                product = None
                for part in parts:
                    term = lax.dot_general(held * part[i:i + 1], depth_hot, NT, preferred_element_type=F32)
                    product = term if product is None else product + term
                src_ref[i] = product.reshape(nx, ny, nz)
        else:
            found = spots(cell, parts, range(first, first + len(amps)), position, count, depth_hot)
            for i, amp in enumerate(amps):
                sums[name, amp] = found[i]

    gather("cell", low, 0, (0, 1, 2, 3), "cell")
    gather("x-", high, 0, (0, 1), "y")
    gather("x+", high, 3, (1,), "y")
    gather("y-", low, 8, (0, 1), "x")
    gather("y+", low, 11, (0,), "x")
    gather("x+y-", high, 8, (1,), "one")
    gather("x-y+", high, 10, (0,), "one")
    sub = iota((8, nz), 0)
    for x in range(-1, nx + 1):
        for c in range(2):
            if c == 0 and x == nx:
                continue
            tail = jnp.zeros((8, nz), F32)
            if x < 0:
                head = sums["x-", c]
                if c == 0:
                    tail = jnp.where(sub == 0, sums["x-y+", 0][0:1], tail)
            elif x == nx:
                head = sums["x+", 1]
                tail = jnp.where(sub == 7, sums["x+y-", 1][0:1], tail)
            else:
                head = src_ref[c, x]
                tail = jnp.where(sub == 7, sums["y-", c][x:x + 1], tail)
                if c == 0:
                    tail = jnp.where(sub == 0, sums["y+", 0][x:x + 1], tail)
            new_ref[c, x + 1] = e_ref[c, x + 1] + cb_ref[c, x + 1] * jnp.concatenate([head, tail], axis=0)
    before = None
    for x in range(-1, nx):
        e = [new_ref[0, x + 1], new_ref[1, x + 1], e_ref[2, x + 1]]
        curl = curl_electric(e, [None, new_ref[1, x + 2], e_ref[2, x + 2]])
        inside = cb_ref[1, x + 1] > 0.0
        h = [jnp.where(inside, h_ref[c, x + 1] - 0.5 * curl[c], 0.0) for c in range(3)]
        if x >= 0:
            drive = curl_magnetic(h, before)
            for c in range(3):
                ca, cb = coefficients(s_ref[c, x])
                push = drive[c][0:ny]
                if c < 2:
                    push = push + src_ref[2 + c, x]
                old = e[c][0:ny]
                after = ca * old + cb * push
                h_out[c, x] = h[c][0:ny]
                e_out[c, x] = after
                g_out[c, x] = fwd_ref[0, c, x].astype(F32) * old + fwd_ref[1, c, x].astype(F32) * after
        before = h


def body(e_adjoint, h_adjoint, sigma, e_forward, misfit, dest_tile, recv_cell, time_weights):
    tiles = lax.axis_size("gx")
    rows = misfit.shape[0]
    grid = e_adjoint.shape
    nx, ny, nz = grid[1:]
    wide = (ny + 8, nz)
    lines = misfit.reshape(rows, 2, 2, 128).transpose(0, 2, 1, 3).reshape(rows * 4, 128)
    message = ((2 * nx + 2, 8, nz), F32)
    fields, up, down = call(
        functools.partial(rows_kernel, rows),
        [lines, dest_tile.reshape(1, rows), recv_cell.reshape(1, rows), time_weights, e_adjoint, h_adjoint, sigma],
        [((8, rows), F32), message, message], name="rows",
    )
    up, down = shift(up, "gy", 1), shift(down, "gy", -1)
    own, = call(functools.partial(own_kernel, tiles), [fields], [((tiles, 8, 128), F32)], flops=4 * 2 * 256 * rows * 128, name="own")
    packed, = call(functools.partial(message_kernel, tiles, nx), [own, up, down], [((tiles, 16, 128), F32)], flops=8 * 2 * 256 * rows * 128, name="message")
    received = lax.all_to_all(packed, "gx", split_axis=0, concat_axis=0, tiled=True)
    halo, right, left = call(
        halo_kernel, [e_adjoint, h_adjoint, sigma, up, down],
        [((9, nx, 8, nz), F32), ((14,) + wide, F32), ((10,) + wide, F32)], name="halo",
    )
    right, left = shift(right, "gx", 1), shift(left, "gx", -1)
    e1, h1, cb = call(
        first_kernel, [e_adjoint, h_adjoint, sigma, halo, right, left],
        [((3, nx + 2) + wide, F32), ((3, nx + 1) + wide, F32), ((2, nx + 2) + wide, F32)], name="first",
    )
    return call(
        functools.partial(final_kernel, tiles), [received, e1, h1, cb, sigma, e_forward],
        [(grid, F32)] * 3,
        scratch=[pltpu.VMEM((4,) + grid[1:], F32), pltpu.VMEM((2, nx + 2) + wide, F32)],
        flops=2 * 8 * 256 * 2048 * 256, name="final",
    )


def solution(mesh):
    placed = (
        P(None, "gx", "gy", None),
        P(None, "gx", "gy", None),
        P(None, "gx", "gy", None),
        P(None, None, "gx", "gy", None),
        P(("gx", "gy"), None, None),
        P(("gx", "gy"), None),
        P(("gx", "gy")),
        P(),
    )
    return jax.shard_map(
        body,
        mesh=mesh,
        in_specs=placed,
        out_specs=(P(None, "gx", "gy", None), P(None, "gx", "gy", None), P(None, "gx", "gy", None)),
        check_vma=False,
    )
```

```python
import functools

import jax
import jax.numpy as jnp
from jax import lax
from jax.experimental import pallas as pl
from jax.experimental.pallas import tpu as pltpu
from jax.sharding import PartitionSpec as P

STEPS = 2
CAP = 48
NT = (((1,), (1,)), ((), ()))
VMEM = pl.BlockSpec(memory_space=pltpu.VMEM)
FAR = pl.BlockSpec(memory_space=pltpu.HBM)
F32 = jnp.float32
BF16 = jnp.bfloat16


def shift(block, axis, distance):
    devices = range(lax.axis_size(axis))
    route = [(i - distance, i) for i in devices if i - distance in devices]
    return lax.ppermute(block, axis, route)


def call(kernel, args, outs, scratch=(), flops=0, name=None, far_in=(), far_out=(), room=16):
    outs = [jax.ShapeDtypeStruct(shape, dtype) for shape, dtype in outs]
    moved = sum(a.size * a.dtype.itemsize for a in list(args) + outs)
    return pl.pallas_call(
        kernel,
        out_shape=outs,
        in_specs=[FAR if i in far_in else VMEM for i in range(len(args))],
        out_specs=[FAR if i in far_out else VMEM for i in range(len(outs))],
        scratch_shapes=list(scratch),
        compiler_params=pltpu.CompilerParams(vmem_limit_bytes=room * 1024 * 1024),
        cost_estimate=pl.CostEstimate(flops=flops, bytes_accessed=moved, transcendentals=0),
        name=name,
    )(*args)


def iota(shape, axis):
    return lax.broadcasted_iota(jnp.int32, shape, axis)


def hot(condition):
    return jnp.where(condition, 1.0, 0.0).astype(BF16)


def pieces(value):
    high = value.astype(BF16)
    return high, (value - high.astype(F32)).astype(BF16)


def turn(a, amount, axis):
    amount = amount % a.shape[axis]
    return a if amount == 0 else pltpu.roll(a, amount, axis)


def z_up(a):
    return jnp.where(iota(a.shape, 1) == a.shape[1] - 1, 0.0, turn(a, -1, 1))


def z_low(a):
    return jnp.where(iota(a.shape, 1) == 0, 0.0, turn(a, 1, 1))


def y_up(a):
    return turn(a, -1, 0)


def y_low(a):
    return turn(a, 1, 0)


def edge_copies(e_hbm, h_hbm, s_hbm, right_ref, left_ref, sems):
    nx = e_hbm.shape[1]
    plan = (
        (e_hbm, nx - 2, 2, right_ref, 0), (h_hbm, nx - 2, 2, right_ref, 2), (s_hbm, nx - 1, 1, right_ref, 4),
        (e_hbm, 0, 2, left_ref, 0), (h_hbm, 0, 1, left_ref, 2), (s_hbm, 0, 1, left_ref, 3),
    )
    return [
        pltpu.make_async_copy(source.at[:, pl.ds(x, count)], target.at[:, pl.ds(first, count)], sems.at[at])
        for at, (source, x, count, target, first) in enumerate(plan)
    ]


def rows_kernel(
    rows, parts, misfit_hbm, dest_hbm, cell_hbm, weights_hbm, e_hbm, h_hbm, s_hbm, own_ref, right_ref, left_ref,
    misfit_ref, dest_ref, cell_ref, weights_ref, sems, edge_sems,
):
    depth = 4 * rows // parts
    copies = [
        pltpu.make_async_copy(dest_hbm, dest_ref, sems.at[parts]),
        pltpu.make_async_copy(weights_hbm, weights_ref, sems.at[parts + 1]),
        pltpu.make_async_copy(cell_hbm, cell_ref, sems.at[parts + 2]),
    ]
    for part in range(parts):
        span = pl.ds(part * depth, depth)
        copies.append(pltpu.make_async_copy(misfit_hbm.at[span], misfit_ref.at[span], sems.at[part]))
    copies.extend(edge_copies(e_hbm, h_hbm, s_hbm, right_ref, left_ref, edge_sems))
    for copy in copies:
        copy.start()
    for copy in copies[0:3]:
        copy.wait()
    weights = weights_ref[...]
    row = iota((8, rows), 0)
    fields = jnp.where(row == 4, cell_ref[...].reshape(1, rows).astype(F32), 0.0)
    fields = jnp.where(row == 5, dest_ref[...].astype(F32), fields)
    own_ref[...] = fields
    for part in range(parts):
        copies[3 + part].wait()
        count = rows // parts
        line = iota((4, count), 0)
        amps = jnp.zeros((4, count), F32)
        for comp in range(2):
            total = None
            for half in range(2):
                block = misfit_ref[pl.ds(part * depth + 2 * half + comp, count, stride=4), :]
                term = lax.dot_general(
                    weights[:, half * 128:(half + 1) * 128], block, NT,
                    precision=lax.Precision.HIGHEST, preferred_element_type=F32,
                )
                total = term if total is None else total + term
            for k in range(STEPS):
                amps = jnp.where(line == 2 * k + comp, total[k:k + 1], amps)
        own_ref[0:4, part * count:(part + 1) * count] = amps
    for copy in copies[3 + parts:]:
        copy.wait()


def plane_of(refs, right_ref, left_ref, field, c, x):
    nx = refs[0].shape[1]
    if 0 <= x < nx:
        return refs[field][c, x]
    at = {(0, -2): 0, (0, -1): 1, (1, -2): 2, (1, -1): 3, (2, -1): 4}.get((field, x))
    if at is not None:
        return right_ref[c, at]
    at = {(0, nx): 0, (0, nx + 1): 1, (1, nx): 2, (2, nx): 3}.get((field, x))
    return None if at is None else left_ref[c, at]


def side_kernel(e_ref, h_ref, s_ref, right_ref, left_ref, up_ref, down_ref):
    nx, nz = e_ref.shape[1], e_ref.shape[3]
    sub = iota((8, nz), 0)
    zero = jnp.zeros((16, nz), F32)
    for x in range(-2, nx + 2):
        planes = [[plane_of((e_ref, h_ref, s_ref), right_ref, left_ref, f, c, x) for c in range(3)] for f in range(3)]
        planes = [[zero if p is None else p for p in group] for group in planes]
        e, h, s = [[p[8:16] for p in group] for group in planes]
        three = [jnp.where(sub < 2, turn(f[0], 2, 0), jnp.where(sub < 4, turn(f[1], 4, 0), turn(f[2], 6, 0))) for f in (e, h)]
        at, other = x + 2, nx + 6 + x
        up_ref[at] = jnp.where(sub < 6, three[0], jnp.where(sub == 6, turn(s[0], 7, 0), s[1]))
        up_ref[other] = jnp.where(sub < 6, three[1], jnp.where(sub == 6, turn(s[2], 7, 0), 0.0))
        e, h, s = [[p[0:8] for p in group] for group in planes]
        three = jnp.where(sub < 2, e[0], jnp.where(sub < 4, turn(e[1], 2, 0), turn(e[2], 4, 0)))
        down_ref[at] = jnp.where(sub < 6, three, jnp.where(sub == 6, turn(s[0], 6, 0), turn(s[1], 7, 0)))
        three = jnp.where(sub == 0, h[0], jnp.where(sub == 1, turn(h[1], 1, 0), turn(h[2], 2, 0)))
        down_ref[other] = jnp.where(sub < 3, three, jnp.where(sub == 3, turn(s[2], 3, 0), 0.0))


def places(fields, tiles):
    rows = fields.shape[1]
    dest = fields[5:6].astype(jnp.int32)
    named = (iota((tiles, rows), 0) == dest).astype(F32)
    before = jnp.dot(named.astype(BF16), hot(iota((rows, rows), 0) < iota((rows, rows), 1)), preferred_element_type=F32)
    slot = jnp.sum(named * before, axis=0, keepdims=True).astype(jnp.int32)
    cell = fields[4:5].astype(jnp.int32)
    return dest, slot, cell // 4096, (cell // 256) % 16


def lay(fields, slot, offset, picks):
    tiles, rows = 32, fields.shape[1]
    row = iota((8, rows), 0)
    left = [jnp.zeros((8, rows), BF16).astype(F32)] * 2
    where = jnp.full((8, rows), -1, jnp.int32)
    for at, field, tile in picks:
        for number, part in enumerate(pieces(fields[field:field + 1])):
            left[number] = jnp.where(row == at, part.astype(F32), left[number])
        where = jnp.where(row == at, tile, where)
    mask = iota((tiles, 8, rows), 0) == where[None]
    spread = hot(iota((128, rows), 0) == slot + offset)
    total = None
    for part in left:
        block = jnp.where(mask, part[None], 0.0).reshape(tiles * 8, rows).astype(BF16)
        product = lax.dot_general(block, spread, NT, preferred_element_type=F32)
        total = product if total is None else total + product
    return total.reshape(tiles, 8, 128)


def own_kernel(tiles, fields_ref, out_ref):
    fields = fields_ref[...]
    dest, slot, x, _ = places(fields, tiles)
    after = jnp.where(x == 15, dest + 1, -1)
    ahead = jnp.where(x == 0, dest - 1, -1)
    out_ref[...] = lay(fields, slot, 0, [(i, i, dest) for i in range(5)]) + lay(
        fields, slot, 64, [(0, 0, after), (1, 1, after), (2, 4, after), (3, 1, ahead), (4, 4, ahead)]
    )


def message_kernel(tiles, own_ref, up_ref, down_ref, out_ref):
    out_ref[:, 0:8] = own_ref[...]
    fields = up_ref[...]
    dest, slot, x, y = places(fields, tiles)
    here = jnp.where(y == 15, dest, -1)
    ahead = jnp.where((y == 15) & (x == 0), dest - 1, -1)
    block = lay(fields, slot, 0, [(0, 0, here), (1, 1, here), (2, 4, here)])
    block = block + lay(fields, slot, 64, [(0, 1, ahead), (1, 4, ahead)])
    fields = down_ref[...]
    dest, slot, x, y = places(fields, tiles)
    here = jnp.where(y == 0, dest, -1)
    after = jnp.where((y == 0) & (x == 15), dest + 1, -1)
    block = block + lay(fields, slot, 0, [(3, 0, here), (4, 4, here)])
    out_ref[:, 8:16] = block + lay(fields, slot, 64, [(2, 0, after), (3, 4, after)])


def coefficients(sigma):
    half = 0.5 * sigma
    under = 1.0 / (1.0 + half)
    return (1.0 - half) * under, 0.5 * under


def curl_electric(e, after):
    ex, ey, ez = e
    cx = (y_up(ez) - ez) - (z_up(ey) - ey)
    cy = (z_up(ex) - ex) - (after[2] - ez)
    cz = (after[1] - ey) - (y_up(ex) - ex)
    return cx, cy, cz


def curl_magnetic(h, before):
    hx, hy, hz = h
    cx = (hz - y_low(hz)) - (hy - z_low(hy))
    cy = (hx - z_low(hx)) - (hz - before[2])
    cz = (hy - before[1]) - (hx - y_low(hx))
    return cx, cy, cz


def spots(cell, table, amps, position, places_, nz_hot):
    held = hot(iota((places_, table[0].shape[1]), 0) == position)
    left = jnp.concatenate([held * part[a:a + 1] for a in amps for part in table], axis=0)
    product = lax.dot_general(left, nz_hot, NT, preferred_element_type=F32)
    n = places_
    return [product[2 * i * n:(2 * i + 1) * n] + product[(2 * i + 1) * n:(2 * i + 2) * n] for i in range(len(amps))]


def scatter_kernel(tiles, recv_ref, src_ref, rim_ref):
    nx, ny, nz = src_ref.shape[1:]
    lane = iota((16, 128), 1)
    low, high = [], []
    for pair in range(tiles // 2):
        one, two = recv_ref[2 * pair], recv_ref[2 * pair + 1]
        low.append(jnp.where(lane < 64, one, turn(two, 64, 1)))
        high.append(jnp.where(lane < 64, turn(one, 64, 1), two))
    sums = []

    def gather(whole, at, amps, kind):
        table = jnp.concatenate([part[8 * (at // 8):8 * (at // 8) + 8] for part in whole], axis=1)
        first = at % 8
        cell = table[first + len(amps):first + len(amps) + 1].astype(jnp.int32)
        depth_hot = hot(iota((nz, table.shape[1]), 0) == cell % nz)
        column = cell // nz
        position, count = {"cell": (column, nx * ny), "x": (column // ny, nx), "y": (column % ny, ny), "one": (column * 0, 16)}[kind]
        parts = pieces(table)
        if kind == "cell":
            held = hot(iota((count, table.shape[1]), 0) == position)
            for i in range(len(amps)):
                product = None
                for part in parts:
                    term = lax.dot_general(held * part[i:i + 1], depth_hot, NT, preferred_element_type=F32)
                    product = term if product is None else product + term
                src_ref[i] = product.reshape(nx, ny, nz)
        else:
            found = spots(cell, parts, range(first, first + len(amps)), position, count, depth_hot)
            sums.extend(found)

    gather(low, 0, (0, 1, 2, 3), "cell")
    gather(high, 0, (0, 1), "y")
    gather(high, 3, (1,), "y")
    gather(low, 8, (0, 1), "x")
    gather(low, 11, (0,), "x")
    gather(high, 8, (1,), "one")
    gather(high, 10, (0,), "one")
    for i, value in enumerate(sums):
        rim_ref[i] = value


def final_kernel(
    e_ref, h_ref, s_ref, right_ref, left_ref, up_ref, down_ref, src_ref, rim_ref, fwd_hbm, e_hbm, h_hbm, g_hbm,
    e1_ref, h1_ref, cb_ref, fwd_ref, e_out, h_out, g_out, sems,
):
    nx, ny, nz = s_ref.shape[1], s_ref.shape[2], s_ref.shape[3]
    fetch = pltpu.make_async_copy(fwd_hbm, fwd_ref, sems.at[0])
    fetch.start()
    sub = iota((8, nz), 0)
    ring = iota((ny + 8, nz), 0)

    def tail_of(field, c, x):
        at = x + 2
        ua, ub, da, db = up_ref[at], up_ref[nx + 4 + at], down_ref[at], down_ref[nx + 4 + at]
        if field == 0:
            return jnp.where(sub < 2, turn(da, -2 * c, 0), jnp.where(sub >= 6, turn(ua, 6 - 2 * c, 0), 0.0))
        if field == 1:
            return jnp.where(sub < 1, turn(db, -c, 0), jnp.where(sub >= 6, turn(ub, 6 - 2 * c, 0), 0.0))
        below, above = ((turn(da, 2, 0), turn(ua, 1, 0)), (turn(da, 1, 0), ua), (turn(db, 5, 0), turn(ub, 1, 0)))[c]
        return jnp.where(sub == 0, below, jnp.where(sub == 7, above, 0.0))

    def plane(field, c, x):
        head = plane_of((e_ref, h_ref, s_ref), right_ref, left_ref, field, c, x)
        return None if head is None else jnp.concatenate([head, tail_of(field, c, x)], axis=0)

    def source(c, x):
        tail = jnp.zeros((8, nz), F32)
        if x < 0:
            if c == 0:
                tail = jnp.where(sub == 0, rim_ref[7, 0:1], tail)
            return jnp.concatenate([rim_ref[c], tail], axis=0)
        if x == nx:
            return jnp.concatenate([rim_ref[2], jnp.where(sub == 7, rim_ref[6, 0:1], tail)], axis=0)
        tail = jnp.where(sub == 7, rim_ref[3 + c, x:x + 1], tail)
        if c == 0:
            tail = jnp.where(sub == 0, rim_ref[5, x:x + 1], tail)
        return jnp.concatenate([src_ref[c, x], tail], axis=0)

    before = None
    now = [plane(0, c, -2) for c in range(3)]
    for x in range(-2, nx + 1):
        e, now = now, [plane(0, c, x + 1) for c in range(3)]
        curl = curl_electric(e, now)
        sigma = [plane(2, c, x) for c in range(3)]
        h = []
        for c in range(3):
            value = plane(1, c, x) - 0.5 * curl[c]
            if x > -2:
                outside = sigma[1] <= 0.0
                value = jnp.where(outside if x == -1 else outside & (ring == ny + 7), 0.0, value)
            h.append(value)
            if -1 <= x < nx:
                h1_ref[c, x + 1] = value
        if x > -2:
            drive = curl_magnetic(h, before)
            for c in range(3):
                ca, cb = coefficients(sigma[c])
                inside = sigma[c] > 0.0
                if c < 2:
                    cb_ref[c, x + 1] = jnp.where(inside, cb, 0.0)
                    if (c, x) != (0, nx):
                        drive_c = drive[c] + source(c, x)
                    else:
                        drive_c = drive[c]
                else:
                    drive_c = drive[c]
                e1_ref[c, x + 1] = jnp.where(inside, ca * e[c] + cb * drive_c, 0.0)
        before = h
    fetch.wait()
    before = None
    sends = []
    for x in range(-1, nx):
        e = [e1_ref[c, x + 1] for c in range(3)]
        curl = curl_electric(e, [e1_ref[c, x + 2] for c in range(3)])
        inside = cb_ref[1, x + 1] > 0.0
        h = [jnp.where(inside, h1_ref[c, x + 1] - 0.5 * curl[c], 0.0) for c in range(3)]
        if x >= 0:
            drive = curl_magnetic(h, before)
            for c in range(3):
                ca, cb = coefficients(s_ref[c, x])
                push = drive[c][0:ny]
                if c < 2:
                    push = push + src_ref[2 + c, x]
                old = e[c][0:ny]
                after = ca * old + cb * push
                h_out[c, x] = h[c][0:ny]
                e_out[c, x] = after
                g_out[c, x] = fwd_ref[0, c, x].astype(F32) * old + fwd_ref[1, c, x].astype(F32) * after
            if x % 4 == 3:
                span = pl.ds(x - 3, 4)
                for near, far in ((e_out, e_hbm), (h_out, h_hbm), (g_out, g_hbm)):
                    sends.append(pltpu.make_async_copy(near.at[:, span], far.at[:, span], sems.at[1 + len(sends)]))
                    sends[-1].start()
        before = h
    for send in sends:
        send.wait()


def body(e_adjoint, h_adjoint, sigma, e_forward, misfit, dest_tile, recv_cell, time_weights):
    tiles = lax.axis_size("gx")
    rows = misfit.shape[0]
    grid = e_adjoint.shape
    nx, ny, nz = grid[1:]
    wide = (ny + 8, nz)
    parts = 3
    lines = misfit.reshape(rows, 2, 2, 128).transpose(0, 2, 1, 3).reshape(rows * 4, 128)
    fields, right, left = call(
        functools.partial(rows_kernel, rows, parts),
        [lines, dest_tile.reshape(1, rows), recv_cell, time_weights, e_adjoint, h_adjoint, sigma],
        [((8, rows), F32), ((3, 5, ny, nz), F32), ((3, 4, ny, nz), F32)],
        scratch=[pltpu.VMEM((rows * 4, 128), F32), pltpu.VMEM((1, rows), jnp.int32), pltpu.VMEM((rows,), jnp.int32),
                 pltpu.VMEM(time_weights.shape, F32), pltpu.SemaphoreType.DMA((parts + 3,)), pltpu.SemaphoreType.DMA((6,))],
        far_in=range(7), name="rows", room=60,
    )
    rows_up, rows_down = shift(fields, "gy", 1), shift(fields, "gy", -1)
    right, left = shift(right, "gx", 1), shift(left, "gx", -1)
    own, = call(functools.partial(own_kernel, tiles), [fields], [((tiles, 8, 128), F32)], flops=4 * 2 * 256 * rows * 128, name="own")
    packed, = call(functools.partial(message_kernel, tiles), [own, rows_up, rows_down], [((tiles, 16, 128), F32)], flops=8 * 2 * 256 * rows * 128, name="message")
    packed, right, left = lax.optimization_barrier((packed, right, left))
    received = lax.all_to_all(packed, "gx", split_axis=0, concat_axis=0, tiled=True)
    side = ((2 * (nx + 4), 8, nz), F32)
    up, down = call(side_kernel, [e_adjoint, h_adjoint, sigma, right, left], [side, side], name="sides")
    up, down = shift(up, "gy", 1), shift(down, "gy", -1)
    source, rim = call(
        functools.partial(scatter_kernel, tiles), [received], [((4,) + grid[1:], F32), ((8, 16, nz), F32)],
        flops=2 * 8 * 256 * 2048 * 256, name="scatter", room=24,
    )
    return call(
        final_kernel, [e_adjoint, h_adjoint, sigma, right, left, up, down, source, rim, e_forward], [(grid, F32)] * 3,
        scratch=[pltpu.VMEM((3, nx + 2) + wide, F32), pltpu.VMEM((3, nx + 1) + wide, F32), pltpu.VMEM((2, nx + 2) + wide, F32),
                 pltpu.VMEM(e_forward.shape, BF16), pltpu.VMEM(grid, F32), pltpu.VMEM(grid, F32), pltpu.VMEM(grid, F32),
                 pltpu.SemaphoreType.DMA((13,))],
        far_in=(9,), far_out=(0, 1, 2), name="final",
    )


def solution(mesh):
    placed = (
        P(None, "gx", "gy", None),
        P(None, "gx", "gy", None),
        P(None, "gx", "gy", None),
        P(None, None, "gx", "gy", None),
        P(("gx", "gy"), None, None),
        P(("gx", "gy"), None),
        P(("gx", "gy")),
        P(),
    )
    return jax.shard_map(
        body,
        mesh=mesh,
        in_specs=placed,
        out_specs=(P(None, "gx", "gy", None), P(None, "gx", "gy", None), P(None, "gx", "gy", None)),
        check_vma=False,
    )
```

```python
import functools

import jax
import jax.numpy as jnp
from jax import lax
from jax.experimental import pallas as pl
from jax.experimental.pallas import tpu as pltpu
from jax.sharding import PartitionSpec as P

STEPS = 2
CAP = 48
NT = (((1,), (1,)), ((), ()))
VMEM = pl.BlockSpec(memory_space=pltpu.VMEM)
FAR = pl.BlockSpec(memory_space=pltpu.HBM)
F32 = jnp.float32
BF16 = jnp.bfloat16


def shift(block, axis, distance):
    count = lax.axis_size(axis)
    return lax.ppermute(block, axis, [(i, (i + distance) % count) for i in range(count)])


def call(kernel, args, outs, scratch=(), flops=0, name=None, far_in=(), far_out=(), room=16):
    outs = [jax.ShapeDtypeStruct(shape, dtype) for shape, dtype in outs]
    moved = sum(a.size * a.dtype.itemsize for a in list(args) + outs)
    return pl.pallas_call(
        kernel,
        out_shape=outs,
        in_specs=[FAR if i in far_in else VMEM for i in range(len(args))],
        out_specs=[FAR if i in far_out else VMEM for i in range(len(outs))],
        scratch_shapes=list(scratch),
        compiler_params=pltpu.CompilerParams(vmem_limit_bytes=room * 1024 * 1024),
        cost_estimate=pl.CostEstimate(flops=flops, bytes_accessed=moved, transcendentals=0),
        name=name,
    )(*args)


def iota(shape, axis):
    return lax.broadcasted_iota(jnp.int32, shape, axis)


def hot(condition):
    return jnp.where(condition, 1.0, 0.0).astype(BF16)


def pieces(value):
    high = value.astype(BF16)
    return high, (value - high.astype(F32)).astype(BF16)


def turn(a, amount, axis):
    amount = amount % a.shape[axis]
    return a if amount == 0 else pltpu.roll(a, amount, axis)


def z_up(a):
    return jnp.where(iota(a.shape, 1) == a.shape[1] - 1, 0.0, turn(a, -1, 1))


def z_low(a):
    return jnp.where(iota(a.shape, 1) == 0, 0.0, turn(a, 1, 1))


def y_up(a):
    return turn(a, -1, 0)


def y_low(a):
    return turn(a, 1, 0)


def clear_ends(axis, onward_ref, back_ref):
    place = lax.axis_index(axis)

    @pl.when(place == lax.axis_size(axis) - 1)
    def _():
        onward_ref[...] = jnp.zeros(onward_ref.shape, F32)

    @pl.when(place == 0)
    def _():
        back_ref[...] = jnp.zeros(back_ref.shape, F32)


def edge_copies(e_hbm, h_hbm, s_hbm, right_ref, left_ref, sems):
    nx = e_hbm.shape[1]
    plan = (
        (e_hbm, nx - 2, 2, right_ref, 0), (h_hbm, nx - 2, 2, right_ref, 2), (s_hbm, nx - 1, 1, right_ref, 4),
        (e_hbm, 0, 2, left_ref, 0), (h_hbm, 0, 1, left_ref, 2), (s_hbm, 0, 1, left_ref, 3),
    )
    return [
        pltpu.make_async_copy(source.at[:, pl.ds(x, count)], target.at[:, pl.ds(first, count)], sems.at[at])
        for at, (source, x, count, target, first) in enumerate(plan)
    ]


def rows_kernel(
    rows, parts, misfit_hbm, dest_hbm, cell_hbm, weights_hbm, e_hbm, h_hbm, s_hbm, own_ref, right_ref, left_ref,
    misfit_ref, dest_ref, cell_ref, weights_ref, sems, edge_sems,
):
    depth = 4 * rows // parts
    copies = [
        pltpu.make_async_copy(dest_hbm, dest_ref, sems.at[parts]),
        pltpu.make_async_copy(weights_hbm, weights_ref, sems.at[parts + 1]),
        pltpu.make_async_copy(cell_hbm, cell_ref, sems.at[parts + 2]),
    ]
    for part in range(parts):
        span = pl.ds(part * depth, depth)
        copies.append(pltpu.make_async_copy(misfit_hbm.at[span], misfit_ref.at[span], sems.at[part]))
    copies.extend(edge_copies(e_hbm, h_hbm, s_hbm, right_ref, left_ref, edge_sems))
    for copy in copies:
        copy.start()
    for copy in copies[0:3]:
        copy.wait()
    weights = weights_ref[...]
    row = iota((8, rows), 0)
    fields = jnp.where(row == 4, cell_ref[...].reshape(1, rows).astype(F32), 0.0)
    fields = jnp.where(row == 5, dest_ref[...].astype(F32), fields)
    own_ref[...] = fields
    for part in range(parts):
        copies[3 + part].wait()
        count = rows // parts
        line = iota((4, count), 0)
        amps = jnp.zeros((4, count), F32)
        for comp in range(2):
            total = None
            for half in range(2):
                block = misfit_ref[pl.ds(part * depth + 2 * half + comp, count, stride=4), :]
                term = lax.dot_general(
                    weights[:, half * 128:(half + 1) * 128], block, NT,
                    precision=lax.Precision.HIGHEST, preferred_element_type=F32,
                )
                total = term if total is None else total + term
            for k in range(STEPS):
                amps = jnp.where(line == 2 * k + comp, total[k:k + 1], amps)
        own_ref[0:4, part * count:(part + 1) * count] = amps
    for copy in copies[3 + parts:]:
        copy.wait()
    clear_ends("gx", right_ref, left_ref)


def plane_of(refs, right_ref, left_ref, field, c, x):
    nx = refs[0].shape[1]
    if 0 <= x < nx:
        return refs[field][c, x]
    at = {(0, -2): 0, (0, -1): 1, (1, -2): 2, (1, -1): 3, (2, -1): 4}.get((field, x))
    if at is not None:
        return right_ref[c, at]
    at = {(0, nx): 0, (0, nx + 1): 1, (1, nx): 2, (2, nx): 3}.get((field, x))
    return None if at is None else left_ref[c, at]


def side_kernel(e_ref, h_ref, s_ref, right_ref, left_ref, up_ref, down_ref):
    nx, nz = e_ref.shape[1], e_ref.shape[3]
    sub = iota((8, nz), 0)
    zero = jnp.zeros((16, nz), F32)
    for x in range(-2, nx + 2):
        planes = [[plane_of((e_ref, h_ref, s_ref), right_ref, left_ref, f, c, x) for c in range(3)] for f in range(3)]
        planes = [[zero if p is None else p for p in group] for group in planes]
        e, h, s = [[p[8:16] for p in group] for group in planes]
        three = [jnp.where(sub < 2, turn(f[0], 2, 0), jnp.where(sub < 4, turn(f[1], 4, 0), turn(f[2], 6, 0))) for f in (e, h)]
        at, other = x + 2, nx + 6 + x
        up_ref[at] = jnp.where(sub < 6, three[0], jnp.where(sub == 6, turn(s[0], 7, 0), s[1]))
        up_ref[other] = jnp.where(sub < 6, three[1], jnp.where(sub == 6, turn(s[2], 7, 0), 0.0))
        e, h, s = [[p[0:8] for p in group] for group in planes]
        three = jnp.where(sub < 2, e[0], jnp.where(sub < 4, turn(e[1], 2, 0), turn(e[2], 4, 0)))
        down_ref[at] = jnp.where(sub < 6, three, jnp.where(sub == 6, turn(s[0], 6, 0), turn(s[1], 7, 0)))
        three = jnp.where(sub == 0, h[0], jnp.where(sub == 1, turn(h[1], 1, 0), turn(h[2], 2, 0)))
        down_ref[other] = jnp.where(sub < 3, three, jnp.where(sub == 3, turn(s[2], 3, 0), 0.0))
    clear_ends("gy", up_ref, down_ref)


def places(fields, tiles):
    rows = fields.shape[1]
    dest = fields[5:6].astype(jnp.int32)
    named = (iota((tiles, rows), 0) == dest).astype(F32)
    before = jnp.dot(named.astype(BF16), hot(iota((rows, rows), 0) < iota((rows, rows), 1)), preferred_element_type=F32)
    slot = jnp.sum(named * before, axis=0, keepdims=True).astype(jnp.int32)
    cell = fields[4:5].astype(jnp.int32)
    return dest, slot, cell // 4096, (cell // 256) % 16


def lay(fields, slot, offset, picks):
    tiles, rows = 32, fields.shape[1]
    row = iota((8, rows), 0)
    left = [jnp.zeros((8, rows), BF16).astype(F32)] * 2
    where = jnp.full((8, rows), -1, jnp.int32)
    for at, field, tile in picks:
        for number, part in enumerate(pieces(fields[field:field + 1])):
            left[number] = jnp.where(row == at, part.astype(F32), left[number])
        where = jnp.where(row == at, tile, where)
    mask = iota((tiles, 8, rows), 0) == where[None]
    spread = hot(iota((128, rows), 0) == slot + offset)
    total = None
    for part in left:
        block = jnp.where(mask, part[None], 0.0).reshape(tiles * 8, rows).astype(BF16)
        product = lax.dot_general(block, spread, NT, preferred_element_type=F32)
        total = product if total is None else total + product
    return total.reshape(tiles, 8, 128)


def own_kernel(tiles, fields_ref, out_ref):
    fields = fields_ref[...]
    dest, slot, x, _ = places(fields, tiles)
    after = jnp.where(x == 15, dest + 1, -1)
    ahead = jnp.where(x == 0, dest - 1, -1)
    out_ref[...] = lay(fields, slot, 0, [(i, i, dest) for i in range(5)]) + lay(
        fields, slot, 64, [(0, 0, after), (1, 1, after), (2, 4, after), (3, 1, ahead), (4, 4, ahead)]
    )


def message_kernel(tiles, own_ref, up_ref, down_ref, out_ref):
    out_ref[:, 0:8] = own_ref[...]
    place = lax.axis_index("gy")
    fields = jnp.where(place > 0, up_ref[...], 0.0)
    dest, slot, x, y = places(fields, tiles)
    here = jnp.where(y == 15, dest, -1)
    ahead = jnp.where((y == 15) & (x == 0), dest - 1, -1)
    block = lay(fields, slot, 0, [(0, 0, here), (1, 1, here), (2, 4, here)])
    block = block + lay(fields, slot, 64, [(0, 1, ahead), (1, 4, ahead)])
    fields = jnp.where(place < lax.axis_size("gy") - 1, down_ref[...], 0.0)
    dest, slot, x, y = places(fields, tiles)
    here = jnp.where(y == 0, dest, -1)
    after = jnp.where((y == 0) & (x == 15), dest + 1, -1)
    block = block + lay(fields, slot, 0, [(3, 0, here), (4, 4, here)])
    out_ref[:, 8:16] = block + lay(fields, slot, 64, [(2, 0, after), (3, 4, after)])


def coefficients(sigma):
    half = 0.5 * sigma
    under = 1.0 / (1.0 + half)
    return (1.0 - half) * under, 0.5 * under


def curl_electric(e, after):
    ex, ey, ez = e
    cx = (y_up(ez) - ez) - (z_up(ey) - ey)
    cy = (z_up(ex) - ex) - (after[2] - ez)
    cz = (after[1] - ey) - (y_up(ex) - ex)
    return cx, cy, cz


def curl_magnetic(h, before):
    hx, hy, hz = h
    cx = (hz - y_low(hz)) - (hy - z_low(hy))
    cy = (hx - z_low(hx)) - (hz - before[2])
    cz = (hy - before[1]) - (hx - y_low(hx))
    return cx, cy, cz


def spots(cell, table, amps, position, places_, nz_hot):
    held = hot(iota((places_, table[0].shape[1]), 0) == position)
    left = jnp.concatenate([held * part[a:a + 1] for a in amps for part in table], axis=0)
    product = lax.dot_general(left, nz_hot, NT, preferred_element_type=F32)
    n = places_
    return [product[2 * i * n:(2 * i + 1) * n] + product[(2 * i + 1) * n:(2 * i + 2) * n] for i in range(len(amps))]


def scatter_kernel(tiles, recv_ref, src_ref, rim_ref):
    nx, ny, nz = src_ref.shape[1:]
    lane = iota((16, 128), 1)
    low, high = [], []
    for pair in range(tiles // 2):
        one, two = recv_ref[2 * pair], recv_ref[2 * pair + 1]
        low.append(jnp.where(lane < 64, one, turn(two, 64, 1)))
        high.append(jnp.where(lane < 64, turn(one, 64, 1), two))
    sums = []

    def gather(whole, at, amps, kind):
        table = jnp.concatenate([part[8 * (at // 8):8 * (at // 8) + 8] for part in whole], axis=1)
        first = at % 8
        cell = table[first + len(amps):first + len(amps) + 1].astype(jnp.int32)
        depth_hot = hot(iota((nz, table.shape[1]), 0) == cell % nz)
        column = cell // nz
        position, count = {"cell": (column, nx * ny), "x": (column // ny, nx), "y": (column % ny, ny), "one": (column * 0, 16)}[kind]
        parts = pieces(table)
        if kind == "cell":
            held = hot(iota((count, table.shape[1]), 0) == position)
            for i in range(len(amps)):
                product = None
                for part in parts:
                    term = lax.dot_general(held * part[i:i + 1], depth_hot, NT, preferred_element_type=F32)
                    product = term if product is None else product + term
                src_ref[i] = product.reshape(nx, ny, nz)
        else:
            found = spots(cell, parts, range(first, first + len(amps)), position, count, depth_hot)
            sums.extend(found)

    gather(low, 0, (0, 1, 2, 3), "cell")
    gather(high, 0, (0, 1), "y")
    gather(high, 3, (1,), "y")
    gather(low, 8, (0, 1), "x")
    gather(low, 11, (0,), "x")
    gather(high, 8, (1,), "one")
    gather(high, 10, (0,), "one")
    for i, value in enumerate(sums):
        rim_ref[i] = value


def final_kernel(
    e_ref, h_ref, s_ref, right_ref, left_ref, up_ref, down_ref, src_ref, rim_ref, fwd_hbm, e_hbm, h_hbm, g_hbm,
    e1_ref, h1_ref, cb_ref, fwd_ref, e_out, h_out, g_out, sems,
):
    nx, ny, nz = s_ref.shape[1], s_ref.shape[2], s_ref.shape[3]
    fetch = pltpu.make_async_copy(fwd_hbm, fwd_ref, sems.at[0])
    fetch.start()
    sub = iota((8, nz), 0)
    ring = iota((ny + 8, nz), 0)

    def tail_of(field, c, x):
        at = x + 2
        ua, ub, da, db = up_ref[at], up_ref[nx + 4 + at], down_ref[at], down_ref[nx + 4 + at]
        if field == 0:
            return jnp.where(sub < 2, turn(da, -2 * c, 0), jnp.where(sub >= 6, turn(ua, 6 - 2 * c, 0), 0.0))
        if field == 1:
            return jnp.where(sub < 1, turn(db, -c, 0), jnp.where(sub >= 6, turn(ub, 6 - 2 * c, 0), 0.0))
        below, above = ((turn(da, 2, 0), turn(ua, 1, 0)), (turn(da, 1, 0), ua), (turn(db, 5, 0), turn(ub, 1, 0)))[c]
        return jnp.where(sub == 0, below, jnp.where(sub == 7, above, 0.0))

    def plane(field, c, x):
        head = plane_of((e_ref, h_ref, s_ref), right_ref, left_ref, field, c, x)
        return None if head is None else jnp.concatenate([head, tail_of(field, c, x)], axis=0)

    def source(c, x):
        tail = jnp.zeros((8, nz), F32)
        if x < 0:
            if c == 0:
                tail = jnp.where(sub == 0, rim_ref[7, 0:1], tail)
            return jnp.concatenate([rim_ref[c], tail], axis=0)
        if x == nx:
            return jnp.concatenate([rim_ref[2], jnp.where(sub == 7, rim_ref[6, 0:1], tail)], axis=0)
        tail = jnp.where(sub == 7, rim_ref[3 + c, x:x + 1], tail)
        if c == 0:
            tail = jnp.where(sub == 0, rim_ref[5, x:x + 1], tail)
        return jnp.concatenate([src_ref[c, x], tail], axis=0)

    before = None
    now = [plane(0, c, -2) for c in range(3)]
    for x in range(-2, nx + 1):
        e, now = now, [plane(0, c, x + 1) for c in range(3)]
        curl = curl_electric(e, now)
        sigma = [plane(2, c, x) for c in range(3)]
        h = []
        for c in range(3):
            value = plane(1, c, x) - 0.5 * curl[c]
            if x > -2:
                outside = sigma[1] <= 0.0
                value = jnp.where(outside if x == -1 else outside & (ring == ny + 7), 0.0, value)
            h.append(value)
            if -1 <= x < nx:
                h1_ref[c, x + 1] = value
        if x > -2:
            drive = curl_magnetic(h, before)
            for c in range(3):
                ca, cb = coefficients(sigma[c])
                inside = sigma[c] > 0.0
                if c < 2:
                    cb_ref[c, x + 1] = jnp.where(inside, cb, 0.0)
                    if (c, x) != (0, nx):
                        drive_c = drive[c] + source(c, x)
                    else:
                        drive_c = drive[c]
                else:
                    drive_c = drive[c]
                e1_ref[c, x + 1] = jnp.where(inside, ca * e[c] + cb * drive_c, 0.0)
        before = h
    fetch.wait()
    before = None
    sends = []
    for x in range(-1, nx):
        e = [e1_ref[c, x + 1] for c in range(3)]
        curl = curl_electric(e, [e1_ref[c, x + 2] for c in range(3)])
        inside = cb_ref[1, x + 1] > 0.0
        h = [jnp.where(inside, h1_ref[c, x + 1] - 0.5 * curl[c], 0.0) for c in range(3)]
        if x >= 0:
            drive = curl_magnetic(h, before)
            for c in range(3):
                ca, cb = coefficients(s_ref[c, x])
                push = drive[c][0:ny]
                if c < 2:
                    push = push + src_ref[2 + c, x]
                old = e[c][0:ny]
                after = ca * old + cb * push
                h_out[c, x] = h[c][0:ny]
                e_out[c, x] = after
                g_out[c, x] = fwd_ref[0, c, x].astype(F32) * old + fwd_ref[1, c, x].astype(F32) * after
            if x % 4 == 3:
                span = pl.ds(x - 3, 4)
                for near, far in ((e_out, e_hbm), (h_out, h_hbm), (g_out, g_hbm)):
                    sends.append(pltpu.make_async_copy(near.at[:, span], far.at[:, span], sems.at[1 + len(sends)]))
                    sends[-1].start()
        before = h
    for send in sends:
        send.wait()


def body(e_adjoint, h_adjoint, sigma, e_forward, misfit, dest_tile, recv_cell, time_weights):
    tiles = lax.axis_size("gx")
    rows = misfit.shape[0]
    grid = e_adjoint.shape
    nx, ny, nz = grid[1:]
    wide = (ny + 8, nz)
    parts = 3
    lines = misfit.reshape(rows, 2, 2, 128).transpose(0, 2, 1, 3).reshape(rows * 4, 128)
    fields, right, left = call(
        functools.partial(rows_kernel, rows, parts),
        [lines, dest_tile.reshape(1, rows), recv_cell, time_weights, e_adjoint, h_adjoint, sigma],
        [((8, rows), F32), ((3, 5, ny, nz), F32), ((3, 4, ny, nz), F32)],
        scratch=[pltpu.VMEM((rows * 4, 128), F32), pltpu.VMEM((1, rows), jnp.int32), pltpu.VMEM((rows,), jnp.int32),
                 pltpu.VMEM(time_weights.shape, F32), pltpu.SemaphoreType.DMA((parts + 3,)), pltpu.SemaphoreType.DMA((6,))],
        far_in=range(7), name="rows", room=60,
    )
    rows_up, rows_down = shift(fields, "gy", 1), shift(fields, "gy", -1)
    right, left = shift(right, "gx", 1), shift(left, "gx", -1)
    own, = call(functools.partial(own_kernel, tiles), [fields], [((tiles, 8, 128), F32)], flops=4 * 2 * 256 * rows * 128, name="own")
    packed, = call(functools.partial(message_kernel, tiles), [own, rows_up, rows_down], [((tiles, 16, 128), F32)], flops=8 * 2 * 256 * rows * 128, name="message")
    packed, right, left = lax.optimization_barrier((packed, right, left))
    received = lax.all_to_all(packed, "gx", split_axis=0, concat_axis=0, tiled=True)
    side = ((2 * (nx + 4), 8, nz), F32)
    up, down = call(side_kernel, [e_adjoint, h_adjoint, sigma, right, left], [side, side], name="sides")
    up, down = shift(up, "gy", 1), shift(down, "gy", -1)
    source, rim = call(
        functools.partial(scatter_kernel, tiles), [received], [((4,) + grid[1:], F32), ((8, 16, nz), F32)],
        flops=2 * 8 * 256 * 2048 * 256, name="scatter", room=24,
    )
    return call(
        final_kernel, [e_adjoint, h_adjoint, sigma, right, left, up, down, source, rim, e_forward], [(grid, F32)] * 3,
        scratch=[pltpu.VMEM((3, nx + 2) + wide, F32), pltpu.VMEM((3, nx + 1) + wide, F32), pltpu.VMEM((2, nx + 2) + wide, F32),
                 pltpu.VMEM(e_forward.shape, BF16), pltpu.VMEM(grid, F32), pltpu.VMEM(grid, F32), pltpu.VMEM(grid, F32),
                 pltpu.SemaphoreType.DMA((13,))],
        far_in=(9,), far_out=(0, 1, 2), name="final",
    )


def solution(mesh):
    placed = (
        P(None, "gx", "gy", None),
        P(None, "gx", "gy", None),
        P(None, "gx", "gy", None),
        P(None, None, "gx", "gy", None),
        P(("gx", "gy"), None, None),
        P(("gx", "gy"), None),
        P(("gx", "gy")),
        P(),
    )
    return jax.shard_map(
        body,
        mesh=mesh,
        in_specs=placed,
        out_specs=(P(None, "gx", "gy", None), P(None, "gx", "gy", None), P(None, "gx", "gy", None)),
        check_vma=False,
    )
```

```python
import functools

import jax
import jax.numpy as jnp
from jax import lax
from jax.experimental import pallas as pl
from jax.experimental.pallas import tpu as pltpu
from jax.sharding import PartitionSpec as P

STEPS = 2
CAP = 48
NT = (((1,), (1,)), ((), ()))
VMEM = pl.BlockSpec(memory_space=pltpu.VMEM)
FAR = pl.BlockSpec(memory_space=pltpu.HBM)
F32 = jnp.float32
BF16 = jnp.bfloat16


def shift(block, axis, distance):
    count = lax.axis_size(axis)
    return lax.ppermute(block, axis, [(i, (i + distance) % count) for i in range(count)])


def call(kernel, args, outs, scratch=(), flops=0, name=None, far_in=(), far_out=(), room=16):
    outs = [jax.ShapeDtypeStruct(shape, dtype) for shape, dtype in outs]
    moved = sum(a.size * a.dtype.itemsize for a in list(args) + outs)
    return pl.pallas_call(
        kernel,
        out_shape=outs,
        in_specs=[FAR if i in far_in else VMEM for i in range(len(args))],
        out_specs=[FAR if i in far_out else VMEM for i in range(len(outs))],
        scratch_shapes=list(scratch),
        compiler_params=pltpu.CompilerParams(vmem_limit_bytes=room * 1024 * 1024),
        cost_estimate=pl.CostEstimate(flops=flops, bytes_accessed=moved, transcendentals=0),
        name=name,
    )(*args)


def iota(shape, axis):
    return lax.broadcasted_iota(jnp.int32, shape, axis)


def hot(condition):
    return jnp.where(condition, 1.0, 0.0).astype(BF16)


def pieces(value):
    high = value.astype(BF16)
    return high, (value - high.astype(F32)).astype(BF16)


def turn(a, amount, axis):
    amount = amount % a.shape[axis]
    return a if amount == 0 else pltpu.roll(a, amount, axis)


def z_up(a):
    return jnp.where(iota(a.shape, 1) == a.shape[1] - 1, 0.0, turn(a, -1, 1))


def z_low(a):
    return jnp.where(iota(a.shape, 1) == 0, 0.0, turn(a, 1, 1))


def y_up(a):
    return turn(a, -1, 0)


def y_low(a):
    return turn(a, 1, 0)


def clear_ends(axis, onward_ref, back_ref):
    place = lax.axis_index(axis)

    @pl.when(place == lax.axis_size(axis) - 1)
    def _():
        onward_ref[...] = jnp.zeros(onward_ref.shape, F32)

    @pl.when(place == 0)
    def _():
        back_ref[...] = jnp.zeros(back_ref.shape, F32)


def edge_copies(e_hbm, h_hbm, s_hbm, right_ref, left_ref, sems):
    nx = e_hbm.shape[1]
    plan = (
        (e_hbm, nx - 2, 2, right_ref, 0), (h_hbm, nx - 2, 2, right_ref, 2), (s_hbm, nx - 1, 1, right_ref, 4),
        (e_hbm, 0, 2, left_ref, 0), (h_hbm, 0, 1, left_ref, 2), (s_hbm, 0, 1, left_ref, 3),
    )
    return [
        pltpu.make_async_copy(source.at[:, pl.ds(x, count)], target.at[:, pl.ds(first, count)], sems.at[at])
        for at, (source, x, count, target, first) in enumerate(plan)
    ]


def rows_kernel(
    rows, parts, misfit_hbm, dest_hbm, cell_hbm, weights_hbm, e_hbm, h_hbm, s_hbm, own_ref, right_ref, left_ref,
    misfit_ref, dest_ref, cell_ref, weights_ref, sems, edge_sems,
):
    depth = 4 * rows // parts
    copies = [
        pltpu.make_async_copy(dest_hbm, dest_ref, sems.at[parts]),
        pltpu.make_async_copy(weights_hbm, weights_ref, sems.at[parts + 1]),
        pltpu.make_async_copy(cell_hbm, cell_ref, sems.at[parts + 2]),
    ]
    for part in range(parts):
        span = pl.ds(part * depth, depth)
        copies.append(pltpu.make_async_copy(misfit_hbm.at[span], misfit_ref.at[span], sems.at[part]))
    copies.extend(edge_copies(e_hbm, h_hbm, s_hbm, right_ref, left_ref, edge_sems))
    for copy in copies:
        copy.start()
    for copy in copies[0:3]:
        copy.wait()
    weights = weights_ref[...]
    row = iota((8, rows), 0)
    fields = jnp.where(row == 4, cell_ref[...].reshape(1, rows).astype(F32), 0.0)
    fields = jnp.where(row == 5, dest_ref[...].astype(F32), fields)
    own_ref[...] = fields
    for part in range(parts):
        copies[3 + part].wait()
        count = rows // parts
        line = iota((4, count), 0)
        amps = jnp.zeros((4, count), F32)
        for comp in range(2):
            total = None
            for half in range(2):
                block = misfit_ref[pl.ds(part * depth + 2 * half + comp, count, stride=4), :]
                term = lax.dot_general(
                    weights[:, half * 128:(half + 1) * 128], block, NT,
                    precision=lax.Precision.HIGHEST, preferred_element_type=F32,
                )
                total = term if total is None else total + term
            for k in range(STEPS):
                amps = jnp.where(line == 2 * k + comp, total[k:k + 1], amps)
        own_ref[0:4, part * count:(part + 1) * count] = amps
    for copy in copies[3 + parts:]:
        copy.wait()
    clear_ends("gx", right_ref, left_ref)


def plane_of(refs, right_ref, left_ref, field, c, x):
    nx = refs[0].shape[1]
    if 0 <= x < nx:
        return refs[field][c, x]
    at = {(0, -2): 0, (0, -1): 1, (1, -2): 2, (1, -1): 3, (2, -1): 4}.get((field, x))
    if at is not None:
        return right_ref[c, at]
    at = {(0, nx): 0, (0, nx + 1): 1, (1, nx): 2, (2, nx): 3}.get((field, x))
    return None if at is None else left_ref[c, at]


def side_kernel(e_ref, h_ref, s_ref, right_ref, left_ref, up_ref, down_ref):
    nx, nz = e_ref.shape[1], e_ref.shape[3]
    sub = iota((8, nz), 0)
    zero = jnp.zeros((16, nz), F32)
    for x in range(-2, nx + 2):
        planes = [[plane_of((e_ref, h_ref, s_ref), right_ref, left_ref, f, c, x) for c in range(3)] for f in range(3)]
        planes = [[zero if p is None else p for p in group] for group in planes]
        e, h, s = [[p[8:16] for p in group] for group in planes]
        three = [jnp.where(sub < 2, turn(f[0], 2, 0), jnp.where(sub < 4, turn(f[1], 4, 0), turn(f[2], 6, 0))) for f in (e, h)]
        at, other = x + 2, nx + 6 + x
        up_ref[at] = jnp.where(sub < 6, three[0], jnp.where(sub == 6, turn(s[0], 7, 0), s[1]))
        up_ref[other] = jnp.where(sub < 6, three[1], jnp.where(sub == 6, turn(s[2], 7, 0), 0.0))
        e, h, s = [[p[0:8] for p in group] for group in planes]
        three = jnp.where(sub < 2, e[0], jnp.where(sub < 4, turn(e[1], 2, 0), turn(e[2], 4, 0)))
        down_ref[at] = jnp.where(sub < 6, three, jnp.where(sub == 6, turn(s[0], 6, 0), turn(s[1], 7, 0)))
        three = jnp.where(sub == 0, h[0], jnp.where(sub == 1, turn(h[1], 1, 0), turn(h[2], 2, 0)))
        down_ref[other] = jnp.where(sub < 3, three, jnp.where(sub == 3, turn(s[2], 3, 0), 0.0))
    clear_ends("gy", up_ref, down_ref)


def parse(fields):
    dest = fields[5:6].astype(jnp.int32)
    cell = fields[4:5].astype(jnp.int32)
    return dest, cell // 4096, (cell // 256) % 16


def ranks(groups, tiles):
    rows = groups[0].shape[1]
    named = [(iota((tiles, rows), 0) == group).astype(F32) for group in groups]
    earlier = hot(iota((rows, rows), 0) < iota((rows, rows), 1))
    before = jnp.dot(jnp.concatenate(named, axis=0).astype(BF16), earlier, preferred_element_type=F32)
    return [
        jnp.sum(one * before[tiles * n:tiles * (n + 1)], axis=0, keepdims=True).astype(jnp.int32) for n, one in enumerate(named)
    ]


def lay(fields, lane, picks):
    tiles, rows = 32, fields.shape[1]
    row = iota((8, rows), 0)
    left = [jnp.zeros((8, rows), BF16).astype(F32)] * 2
    where = jnp.full((8, rows), -1, jnp.int32)
    for at, field, tile in picks:
        for number, part in enumerate(pieces(fields[field:field + 1])):
            left[number] = jnp.where(row == at, part.astype(F32), left[number])
        where = jnp.where(row == at, tile, where)
    mask = iota((tiles, 8, rows), 0) == where[None]
    spread = hot(iota((128, rows), 0) == lane)
    total = None
    for part in left:
        block = jnp.where(mask, part[None], 0.0).reshape(tiles * 8, rows).astype(BF16)
        product = lax.dot_general(block, spread, NT, preferred_element_type=F32)
        total = product if total is None else total + product
    return total.reshape(tiles, 8, 128)


def corner_picks(rank, field, tile):
    picks = []
    for group in range(3):
        here = jnp.where(rank // 16 == group, tile, -1)
        picks += [(2 * group, field, here), (2 * group + 1, 4, here)]
    return picks


def own_kernel(tiles, fields_ref, out_ref):
    fields = fields_ref[...]
    dest, x, _ = parse(fields)
    after = jnp.where(x == 15, dest + 1, -1)
    ahead = jnp.where(x == 0, dest - 1, -1)
    slot, rank_after, rank_ahead = ranks([dest, after, ahead], tiles)
    block = lay(fields, slot, [(i, i, dest) for i in range(5)])
    block = block + lay(fields, rank_after + 64, [(0, 0, after), (1, 1, after), (2, 4, after)])
    out_ref[...] = block + lay(fields, rank_ahead + 64, [(3, 1, ahead), (4, 4, ahead)])


def message_kernel(tiles, own_ref, up_ref, down_ref, out_ref):
    place = lax.axis_index("gy")
    fields = jnp.where(place > 0, up_ref[...], 0.0)
    dest, x, y = parse(fields)
    here = jnp.where(y == 15, dest, -1)
    ahead = jnp.where((y == 15) & (x == 0), dest - 1, -1)
    rank, corner = ranks([here, ahead], tiles)
    block = own_ref[...] + lay(fields, rank, [(5, 0, here), (6, 1, here), (7, 4, here)])
    block = block + lay(fields, 48 + corner % 16, corner_picks(corner, 1, ahead))
    fields = jnp.where(place < lax.axis_size("gy") - 1, down_ref[...], 0.0)
    dest, x, y = parse(fields)
    filled = (fields[0:1] != 0.0) | (fields[1:2] != 0.0) | (fields[2:3] != 0.0) | (fields[3:4] != 0.0)
    here = jnp.where((y == 0) & filled, dest, -1)
    after = jnp.where((y == 0) & (x == 15) & filled, dest + 1, -1)
    rank, corner = ranks([here, after], tiles)
    block = block + lay(fields, rank + 64, [(5, 0, here), (6, 4, here)])
    out_ref[...] = block + lay(fields, 112 + corner % 16, corner_picks(corner, 0, after))


def coefficients(sigma):
    half = 0.5 * sigma
    under = 1.0 / (1.0 + half)
    return (1.0 - half) * under, 0.5 * under


def curl_electric(e, after):
    ex, ey, ez = e
    cx = (y_up(ez) - ez) - (z_up(ey) - ey)
    cy = (z_up(ex) - ex) - (after[2] - ez)
    cz = (after[1] - ey) - (y_up(ex) - ex)
    return cx, cy, cz


def curl_magnetic(h, before):
    hx, hy, hz = h
    cx = (hz - y_low(hz)) - (hy - z_low(hy))
    cy = (hx - z_low(hx)) - (hz - before[2])
    cz = (hy - before[1]) - (hx - y_low(hx))
    return cx, cy, cz


def listed(table, amps, cell_row, position, count, nz):
    cell = table[cell_row:cell_row + 1].astype(jnp.int32)
    depth_hot = hot(iota((nz, table.shape[1]), 0) == cell % nz)
    held = hot(iota((count, table.shape[1]), 0) == position(cell // nz))
    left = jnp.concatenate([held * part[a:a + 1] for a in amps for part in pieces(table)], axis=0)
    product = lax.dot_general(left, depth_hot, NT, preferred_element_type=F32)
    return [
        product[2 * i * count:(2 * i + 1) * count] + product[(2 * i + 1) * count:(2 * i + 2) * count] for i in range(len(amps))
    ]


def scatter_kernel(tiles, recv_ref, src_ref, rim_ref):
    nx, ny, nz = src_ref.shape[1:]
    lane = iota((8, 128), 1)
    row = iota((8, tiles * 16), 0)

    def group(number):
        out = []
        for first in range(0, tiles, 8):
            merged = None
            for at in range(8):
                moved = turn(recv_ref[first + at], 16 * (at - number), 1)
                merged = moved if merged is None else jnp.where(lane // 16 == at, moved, merged)
            out.append(merged)
        return jnp.concatenate(out, axis=1)

    groups = [group(number) for number in range(8)]
    table = jnp.concatenate(groups[0:3], axis=1)
    depth = table.shape[1]
    cell = table[4:5].astype(jnp.int32)
    column_hot = hot(iota((nx * ny, depth), 0) == cell // nz)
    depth_hot = hot(iota((nz, depth), 0) == cell % nz)
    parts = pieces(table)
    for i in range(4):
        product = None
        for part in parts:
            term = lax.dot_general(column_hot * part[i:i + 1], depth_hot, NT, preferred_element_type=F32)
            product = term if product is None else product + term
        src_ref[i] = product.reshape(nx, ny, nz)

    def rim(q):
        sums = listed(groups[4 + q], (0, 1), 2, lambda column: column % ny, ny, nz)
        sums += listed(groups[4 + q], (3,), 4, lambda column: column % ny, ny, nz)
        sums += listed(groups[q], (5, 6), 7, lambda column: column // ny, nx, nz)
        sums += listed(groups[4 + q], (5,), 6, lambda column: column // ny, nx, nz)
        sums += listed(groups[3], (2 * q,), 2 * q + 1, lambda column: column * 0, 16, nz)
        return sums + listed(groups[7], (2 * q,), 2 * q + 1, lambda column: column * 0, 16, nz)

    for i, value in enumerate(rim(0)):
        rim_ref[i] = value
    more = jnp.where(row >= 5, jnp.abs(groups[1]) + jnp.abs(groups[2]), 0.0)
    more = more + jnp.where(row < 7, jnp.abs(groups[5]) + jnp.abs(groups[6]), 0.0)
    more = more + jnp.where((row >= 2) & (row < 6), jnp.abs(groups[3]) + jnp.abs(groups[7]), 0.0)

    @pl.when(jnp.max(more) > 0.0)
    def _():
        for q in (1, 2):
            for i, value in enumerate(rim(q)):
                rim_ref[i] += value


def final_kernel(
    e_ref, h_ref, s_ref, right_ref, left_ref, up_ref, down_ref, src_ref, rim_ref, fwd_hbm, e_hbm, h_hbm, g_hbm,
    e1_ref, h1_ref, cb_ref, fwd_ref, e_out, h_out, g_out, sems,
):
    nx, ny, nz = s_ref.shape[1], s_ref.shape[2], s_ref.shape[3]
    fetch = pltpu.make_async_copy(fwd_hbm, fwd_ref, sems.at[0])
    fetch.start()
    sub = iota((8, nz), 0)
    ring = iota((ny + 8, nz), 0)

    def tail_of(field, c, x):
        at = x + 2
        ua, ub, da, db = up_ref[at], up_ref[nx + 4 + at], down_ref[at], down_ref[nx + 4 + at]
        if field == 0:
            return jnp.where(sub < 2, turn(da, -2 * c, 0), jnp.where(sub >= 6, turn(ua, 6 - 2 * c, 0), 0.0))
        if field == 1:
            return jnp.where(sub < 1, turn(db, -c, 0), jnp.where(sub >= 6, turn(ub, 6 - 2 * c, 0), 0.0))
        below, above = ((turn(da, 2, 0), turn(ua, 1, 0)), (turn(da, 1, 0), ua), (turn(db, 5, 0), turn(ub, 1, 0)))[c]
        return jnp.where(sub == 0, below, jnp.where(sub == 7, above, 0.0))

    def plane(field, c, x):
        head = plane_of((e_ref, h_ref, s_ref), right_ref, left_ref, field, c, x)
        return None if head is None else jnp.concatenate([head, tail_of(field, c, x)], axis=0)

    def source(c, x):
        tail = jnp.zeros((8, nz), F32)
        if x < 0:
            if c == 0:
                tail = jnp.where(sub == 0, rim_ref[7, 0:1], tail)
            return jnp.concatenate([rim_ref[c], tail], axis=0)
        if x == nx:
            return jnp.concatenate([rim_ref[2], jnp.where(sub == 7, rim_ref[6, 0:1], tail)], axis=0)
        tail = jnp.where(sub == 7, rim_ref[3 + c, x:x + 1], tail)
        if c == 0:
            tail = jnp.where(sub == 0, rim_ref[5, x:x + 1], tail)
        return jnp.concatenate([src_ref[c, x], tail], axis=0)

    before = None
    now = [plane(0, c, -2) for c in range(3)]
    for x in range(-2, nx + 1):
        e, now = now, [plane(0, c, x + 1) for c in range(3)]
        curl = curl_electric(e, now)
        sigma = [plane(2, c, x) for c in range(3)]
        h = []
        for c in range(3):
            value = plane(1, c, x) - 0.5 * curl[c]
            if x > -2:
                outside = sigma[1] <= 0.0
                value = jnp.where(outside if x == -1 else outside & (ring == ny + 7), 0.0, value)
            h.append(value)
            if -1 <= x < nx:
                h1_ref[c, x + 1] = value
        if x > -2:
            drive = curl_magnetic(h, before)
            for c in range(3):
                ca, cb = coefficients(sigma[c])
                inside = sigma[c] > 0.0
                if c < 2:
                    cb_ref[c, x + 1] = jnp.where(inside, cb, 0.0)
                    if (c, x) != (0, nx):
                        drive_c = drive[c] + source(c, x)
                    else:
                        drive_c = drive[c]
                else:
                    drive_c = drive[c]
                e1_ref[c, x + 1] = jnp.where(inside, ca * e[c] + cb * drive_c, 0.0)
        before = h
    fetch.wait()
    before = None
    sends = []
    for x in range(-1, nx):
        e = [e1_ref[c, x + 1] for c in range(3)]
        curl = curl_electric(e, [e1_ref[c, x + 2] for c in range(3)])
        inside = cb_ref[1, x + 1] > 0.0
        h = [jnp.where(inside, h1_ref[c, x + 1] - 0.5 * curl[c], 0.0) for c in range(3)]
        if x >= 0:
            drive = curl_magnetic(h, before)
            for c in range(3):
                ca, cb = coefficients(s_ref[c, x])
                push = drive[c][0:ny]
                if c < 2:
                    push = push + src_ref[2 + c, x]
                old = e[c][0:ny]
                after = ca * old + cb * push
                h_out[c, x] = h[c][0:ny]
                e_out[c, x] = after
                g_out[c, x] = fwd_ref[0, c, x].astype(F32) * old + fwd_ref[1, c, x].astype(F32) * after
            if x % 4 == 3:
                span = pl.ds(x - 3, 4)
                for near, far in ((e_out, e_hbm), (h_out, h_hbm), (g_out, g_hbm)):
                    sends.append(pltpu.make_async_copy(near.at[:, span], far.at[:, span], sems.at[1 + len(sends)]))
                    sends[-1].start()
        before = h
    for send in sends:
        send.wait()


def body(e_adjoint, h_adjoint, sigma, e_forward, misfit, dest_tile, recv_cell, time_weights):
    tiles = lax.axis_size("gx")
    rows = misfit.shape[0]
    grid = e_adjoint.shape
    nx, ny, nz = grid[1:]
    wide = (ny + 8, nz)
    parts = 3
    lines = misfit.reshape(rows, 2, 2, 128).transpose(0, 2, 1, 3).reshape(rows * 4, 128)
    fields, right, left = call(
        functools.partial(rows_kernel, rows, parts),
        [lines, dest_tile.reshape(1, rows), recv_cell, time_weights, e_adjoint, h_adjoint, sigma],
        [((8, rows), F32), ((3, 5, ny, nz), F32), ((3, 4, ny, nz), F32)],
        scratch=[pltpu.VMEM((rows * 4, 128), F32), pltpu.VMEM((1, rows), jnp.int32), pltpu.VMEM((rows,), jnp.int32),
                 pltpu.VMEM(time_weights.shape, F32), pltpu.SemaphoreType.DMA((parts + 3,)), pltpu.SemaphoreType.DMA((6,))],
        far_in=range(7), name="rows", room=58,
    )
    rows_up, rows_down = shift(fields, "gy", 1), shift(fields, "gy", -1)
    right, left = shift(right, "gx", 1), shift(left, "gx", -1)
    own, = call(functools.partial(own_kernel, tiles), [fields], [((tiles, 8, 128), F32)], flops=4 * 2 * 256 * rows * 128, name="own")
    packed, = call(functools.partial(message_kernel, tiles), [own, rows_up, rows_down], [((tiles, 8, 128), F32)], flops=8 * 2 * 256 * rows * 128, name="message")
    packed, right, left = lax.optimization_barrier((packed, right, left))
    received = lax.all_to_all(packed, "gx", split_axis=0, concat_axis=0, tiled=True)
    side = ((2 * (nx + 4), 8, nz), F32)
    up, down = call(side_kernel, [e_adjoint, h_adjoint, sigma, right, left], [side, side], name="sides")
    up, down = shift(up, "gy", 1), shift(down, "gy", -1)
    source, rim = call(
        functools.partial(scatter_kernel, tiles), [received], [((4,) + grid[1:], F32), ((8, 16, nz), F32)],
        flops=2 * 8 * 256 * 2048 * 256, name="scatter", room=24,
    )
    return call(
        final_kernel, [e_adjoint, h_adjoint, sigma, right, left, up, down, source, rim, e_forward], [(grid, F32)] * 3,
        scratch=[pltpu.VMEM((3, nx + 2) + wide, F32), pltpu.VMEM((3, nx + 1) + wide, F32), pltpu.VMEM((2, nx + 2) + wide, F32),
                 pltpu.VMEM(e_forward.shape, BF16), pltpu.VMEM(grid, F32), pltpu.VMEM(grid, F32), pltpu.VMEM(grid, F32),
                 pltpu.SemaphoreType.DMA((13,))],
        far_in=(9,), far_out=(0, 1, 2), name="final",
    )


def solution(mesh):
    placed = (
        P(None, "gx", "gy", None),
        P(None, "gx", "gy", None),
        P(None, "gx", "gy", None),
        P(None, None, "gx", "gy", None),
        P(("gx", "gy"), None, None),
        P(("gx", "gy"), None),
        P(("gx", "gy")),
        P(),
    )
    return jax.shard_map(
        body,
        mesh=mesh,
        in_specs=placed,
        out_specs=(P(None, "gx", "gy", None), P(None, "gx", "gy", None), P(None, "gx", "gy", None)),
        check_vma=False,
    )
```

```python
import functools

import jax
import jax.numpy as jnp
from jax import lax
from jax.experimental import pallas as pl
from jax.experimental.pallas import tpu as pltpu
from jax.sharding import PartitionSpec as P

STEPS = 2
CAP = 48
NT = (((1,), (1,)), ((), ()))
VMEM = pl.BlockSpec(memory_space=pltpu.VMEM)
FAR = pl.BlockSpec(memory_space=pltpu.HBM)
F32 = jnp.float32
BF16 = jnp.bfloat16


def shift(block, axis, distance):
    count = lax.axis_size(axis)
    return lax.ppermute(block, axis, [(i, (i + distance) % count) for i in range(count)])


def call(kernel, args, outs, scratch=(), flops=0, name=None, far_in=(), far_out=(), room=16):
    outs = [jax.ShapeDtypeStruct(shape, dtype) for shape, dtype in outs]
    moved = sum(a.size * a.dtype.itemsize for a in list(args) + outs)
    return pl.pallas_call(
        kernel,
        out_shape=outs,
        in_specs=[FAR if i in far_in else VMEM for i in range(len(args))],
        out_specs=[FAR if i in far_out else VMEM for i in range(len(outs))],
        scratch_shapes=list(scratch),
        compiler_params=pltpu.CompilerParams(vmem_limit_bytes=room * 1024 * 1024),
        cost_estimate=pl.CostEstimate(flops=flops, bytes_accessed=moved, transcendentals=0),
        name=name,
    )(*args)


def iota(shape, axis):
    return lax.broadcasted_iota(jnp.int32, shape, axis)


def hot(condition):
    return jnp.where(condition, 1.0, 0.0).astype(BF16)


def pieces(value):
    high = value.astype(BF16)
    return high, (value - high.astype(F32)).astype(BF16)


def turn(a, amount, axis):
    amount = amount % a.shape[axis]
    return a if amount == 0 else pltpu.roll(a, amount, axis)


def z_up(a):
    return jnp.where(iota(a.shape, 1) == a.shape[1] - 1, 0.0, turn(a, -1, 1))


def z_low(a):
    return jnp.where(iota(a.shape, 1) == 0, 0.0, turn(a, 1, 1))


def y_up(a):
    return turn(a, -1, 0)


def y_low(a):
    return turn(a, 1, 0)


def clear_ends(axis, onward_ref, back_ref):
    place = lax.axis_index(axis)

    @pl.when(place == lax.axis_size(axis) - 1)
    def _():
        onward_ref[...] = jnp.zeros(onward_ref.shape, F32)

    @pl.when(place == 0)
    def _():
        back_ref[...] = jnp.zeros(back_ref.shape, F32)


def edge_copies(e_hbm, h_hbm, s_hbm, right_ref, left_ref, sems):
    nx = e_hbm.shape[1]
    plan = (
        (e_hbm, nx - 2, 2, right_ref, 0), (h_hbm, nx - 2, 2, right_ref, 2), (s_hbm, nx - 1, 1, right_ref, 4),
        (e_hbm, 0, 2, left_ref, 0), (h_hbm, 0, 1, left_ref, 2), (s_hbm, 0, 1, left_ref, 3),
    )
    return [
        pltpu.make_async_copy(source.at[:, pl.ds(x, count)], target.at[:, pl.ds(first, count)], sems.at[at])
        for at, (source, x, count, target, first) in enumerate(plan)
    ]


def rows_kernel(
    rows, parts, misfit_hbm, dest_hbm, cell_hbm, weights_hbm, e_hbm, h_hbm, s_hbm, own_ref, right_ref, left_ref,
    misfit_ref, dest_ref, cell_ref, weights_ref, sems, edge_sems,
):
    depth = 4 * rows // parts
    copies = [
        pltpu.make_async_copy(dest_hbm, dest_ref, sems.at[parts]),
        pltpu.make_async_copy(weights_hbm, weights_ref, sems.at[parts + 1]),
        pltpu.make_async_copy(cell_hbm, cell_ref, sems.at[parts + 2]),
    ]
    for part in range(parts):
        span = pl.ds(part * depth, depth)
        copies.append(pltpu.make_async_copy(misfit_hbm.at[span], misfit_ref.at[span], sems.at[part]))
    copies.extend(edge_copies(e_hbm, h_hbm, s_hbm, right_ref, left_ref, edge_sems))
    for copy in copies:
        copy.start()
    for copy in copies[0:3]:
        copy.wait()
    rest = weights_ref[...]
    stack = []
    for _ in range(3):
        stack.append(rest.astype(BF16).astype(F32))
        rest = rest - stack[-1]
    stacked = jnp.concatenate(stack + [jnp.zeros((10, rest.shape[1]), F32)], axis=0).astype(BF16)
    row = iota((8, rows), 0)
    fields = jnp.where(row == 4, cell_ref[...].reshape(1, rows).astype(F32), 0.0)
    fields = jnp.where(row == 5, dest_ref[...].astype(F32), fields)
    own_ref[...] = fields
    for part in range(parts):
        copies[3 + part].wait()
        count = rows // parts
        line = iota((4, count), 0)
        amps = jnp.zeros((4, count), F32)
        for comp in range(2):
            start = part * depth + comp
            block = jnp.concatenate([misfit_ref[pl.ds(start + 2 * half, count, stride=4), :] for half in range(2)], axis=1)
            high, low = [lax.dot_general(stacked, piece, NT, preferred_element_type=F32) for piece in pieces(block)]
            for k in range(STEPS):
                amp = high[k:k + 1] + (high[2 + k:3 + k] + low[k:k + 1]) + (high[4 + k:5 + k] + low[2 + k:3 + k])
                amps = jnp.where(line == 2 * k + comp, amp, amps)
        own_ref[0:4, part * count:(part + 1) * count] = amps
    for copy in copies[3 + parts:]:
        copy.wait()
    clear_ends("gx", right_ref, left_ref)


def plane_of(refs, right_ref, left_ref, field, c, x):
    nx = refs[0].shape[1]
    if 0 <= x < nx:
        return refs[field][c, x]
    at = {(0, -2): 0, (0, -1): 1, (1, -2): 2, (1, -1): 3, (2, -1): 4}.get((field, x))
    if at is not None:
        return right_ref[c, at]
    at = {(0, nx): 0, (0, nx + 1): 1, (1, nx): 2, (2, nx): 3}.get((field, x))
    return None if at is None else left_ref[c, at]


def side_kernel(e_ref, h_ref, s_ref, right_ref, left_ref, up_ref, down_ref):
    nx, nz = e_ref.shape[1], e_ref.shape[3]
    sub = iota((8, nz), 0)
    zero = jnp.zeros((16, nz), F32)
    for x in range(-2, nx + 2):
        planes = [[plane_of((e_ref, h_ref, s_ref), right_ref, left_ref, f, c, x) for c in range(3)] for f in range(3)]
        planes = [[zero if p is None else p for p in group] for group in planes]
        e, h, s = [[p[8:16] for p in group] for group in planes]
        three = [jnp.where(sub < 2, turn(f[0], 2, 0), jnp.where(sub < 4, turn(f[1], 4, 0), turn(f[2], 6, 0))) for f in (e, h)]
        at, other = x + 2, nx + 6 + x
        up_ref[at] = jnp.where(sub < 6, three[0], jnp.where(sub == 6, turn(s[0], 7, 0), s[1]))
        up_ref[other] = jnp.where(sub < 6, three[1], jnp.where(sub == 6, turn(s[2], 7, 0), 0.0))
        e, h, s = [[p[0:8] for p in group] for group in planes]
        three = jnp.where(sub < 2, e[0], jnp.where(sub < 4, turn(e[1], 2, 0), turn(e[2], 4, 0)))
        down_ref[at] = jnp.where(sub < 6, three, jnp.where(sub == 6, turn(s[0], 6, 0), turn(s[1], 7, 0)))
        three = jnp.where(sub == 0, h[0], jnp.where(sub == 1, turn(h[1], 1, 0), turn(h[2], 2, 0)))
        down_ref[other] = jnp.where(sub < 3, three, jnp.where(sub == 3, turn(s[2], 3, 0), 0.0))
    clear_ends("gy", up_ref, down_ref)


def parse(fields):
    dest = fields[5:6].astype(jnp.int32)
    cell = fields[4:5].astype(jnp.int32)
    return dest, cell // 4096, (cell // 256) % 16


def ranks(groups, tiles):
    rows = groups[0].shape[1]
    named = [(iota((tiles, rows), 0) == group).astype(F32) for group in groups]
    earlier = hot(iota((rows, rows), 0) < iota((rows, rows), 1))
    before = jnp.dot(jnp.concatenate(named, axis=0).astype(BF16), earlier, preferred_element_type=F32)
    return [
        jnp.sum(one * before[tiles * n:tiles * (n + 1)], axis=0, keepdims=True).astype(jnp.int32) for n, one in enumerate(named)
    ]


def lay(fields, lane, picks):
    tiles, rows = 32, fields.shape[1]
    row = iota((8, rows), 0)
    left = [jnp.zeros((8, rows), BF16).astype(F32)] * 2
    where = jnp.full((8, rows), -1, jnp.int32)
    for at, field, tile in picks:
        for number, part in enumerate(pieces(fields[field:field + 1])):
            left[number] = jnp.where(row == at, part.astype(F32), left[number])
        where = jnp.where(row == at, tile, where)
    mask = iota((tiles, 8, rows), 0) == where[None]
    spread = hot(iota((128, rows), 0) == lane)
    total = None
    for part in left:
        block = jnp.where(mask, part[None], 0.0).reshape(tiles * 8, rows).astype(BF16)
        product = lax.dot_general(block, spread, NT, preferred_element_type=F32)
        total = product if total is None else total + product
    return total.reshape(tiles, 8, 128)


def corner_picks(rank, field, tile):
    picks = []
    for group in range(3):
        here = jnp.where(rank // 16 == group, tile, -1)
        picks += [(2 * group, field, here), (2 * group + 1, 4, here)]
    return picks


def own_kernel(tiles, fields_ref, out_ref):
    fields = fields_ref[...]
    dest, x, _ = parse(fields)
    after = jnp.where(x == 15, dest + 1, -1)
    ahead = jnp.where(x == 0, dest - 1, -1)
    slot, rank_after, rank_ahead = ranks([dest, after, ahead], tiles)
    block = lay(fields, slot, [(i, i, dest) for i in range(5)])
    block = block + lay(fields, rank_after + 64, [(0, 0, after), (1, 1, after), (2, 4, after)])
    out_ref[...] = block + lay(fields, rank_ahead + 64, [(3, 1, ahead), (4, 4, ahead)])


def message_kernel(tiles, own_ref, up_ref, down_ref, out_ref):
    place = lax.axis_index("gy")
    fields = jnp.where(place > 0, up_ref[...], 0.0)
    dest, x, y = parse(fields)
    here = jnp.where(y == 15, dest, -1)
    ahead = jnp.where((y == 15) & (x == 0), dest - 1, -1)
    rank, corner = ranks([here, ahead], tiles)
    block = own_ref[...] + lay(fields, rank, [(5, 0, here), (6, 1, here), (7, 4, here)])
    block = block + lay(fields, 48 + corner % 16, corner_picks(corner, 1, ahead))
    fields = jnp.where(place < lax.axis_size("gy") - 1, down_ref[...], 0.0)
    dest, x, y = parse(fields)
    filled = (fields[0:1] != 0.0) | (fields[1:2] != 0.0) | (fields[2:3] != 0.0) | (fields[3:4] != 0.0)
    here = jnp.where((y == 0) & filled, dest, -1)
    after = jnp.where((y == 0) & (x == 15) & filled, dest + 1, -1)
    rank, corner = ranks([here, after], tiles)
    block = block + lay(fields, rank + 64, [(5, 0, here), (6, 4, here)])
    out_ref[...] = block + lay(fields, 112 + corner % 16, corner_picks(corner, 0, after))


def coefficients(sigma):
    half = 0.5 * sigma
    under = 1.0 / (1.0 + half)
    return (1.0 - half) * under, 0.5 * under


def curl_electric(e, after):
    ex, ey, ez = e
    cx = (y_up(ez) - ez) - (z_up(ey) - ey)
    cy = (z_up(ex) - ex) - (after[2] - ez)
    cz = (after[1] - ey) - (y_up(ex) - ex)
    return cx, cy, cz


def curl_magnetic(h, before):
    hx, hy, hz = h
    cx = (hz - y_low(hz)) - (hy - z_low(hy))
    cy = (hx - z_low(hx)) - (hz - before[2])
    cz = (hy - before[1]) - (hx - y_low(hx))
    return cx, cy, cz


def listed(table, amps, cell_row, position, count, nz):
    cell = table[cell_row:cell_row + 1].astype(jnp.int32)
    depth_hot = hot(iota((nz, table.shape[1]), 0) == cell % nz)
    held = hot(iota((count, table.shape[1]), 0) == position(cell // nz))
    left = jnp.concatenate([held * part[a:a + 1] for a in amps for part in pieces(table)], axis=0)
    product = lax.dot_general(left, depth_hot, NT, preferred_element_type=F32)
    return [
        product[2 * i * count:(2 * i + 1) * count] + product[(2 * i + 1) * count:(2 * i + 2) * count] for i in range(len(amps))
    ]


def scatter_kernel(tiles, recv_ref, src_ref, rim_ref):
    nx, ny, nz = src_ref.shape[1:]
    lane = iota((8, 128), 1)
    row = iota((8, tiles * 16), 0)

    def group(number):
        out = []
        for first in range(0, tiles, 8):
            merged = None
            for at in range(8):
                moved = turn(recv_ref[first + at], 16 * (at - number), 1)
                merged = moved if merged is None else jnp.where(lane // 16 == at, moved, merged)
            out.append(merged)
        return jnp.concatenate(out, axis=1)

    groups = [group(number) for number in range(8)]
    table = jnp.concatenate(groups[0:3], axis=1)
    depth = table.shape[1]
    cell = table[4:5].astype(jnp.int32)
    column_hot = hot(iota((nx * ny, depth), 0) == cell // nz)
    depth_hot = hot(iota((nz, depth), 0) == cell % nz)
    parts = pieces(table)
    for i in range(4):
        product = None
        for part in parts:
            term = lax.dot_general(column_hot * part[i:i + 1], depth_hot, NT, preferred_element_type=F32)
            product = term if product is None else product + term
        src_ref[i] = product.reshape(nx, ny, nz)

    def rim(q):
        sums = listed(groups[4 + q], (0, 1), 2, lambda column: column % ny, ny, nz)
        sums += listed(groups[4 + q], (3,), 4, lambda column: column % ny, ny, nz)
        sums += listed(groups[q], (5, 6), 7, lambda column: column // ny, nx, nz)
        sums += listed(groups[4 + q], (5,), 6, lambda column: column // ny, nx, nz)
        sums += listed(groups[3], (2 * q,), 2 * q + 1, lambda column: column * 0, 16, nz)
        return sums + listed(groups[7], (2 * q,), 2 * q + 1, lambda column: column * 0, 16, nz)

    for i, value in enumerate(rim(0)):
        rim_ref[i] = value
    more = jnp.where(row >= 5, jnp.abs(groups[1]) + jnp.abs(groups[2]), 0.0)
    more = more + jnp.where(row < 7, jnp.abs(groups[5]) + jnp.abs(groups[6]), 0.0)
    more = more + jnp.where((row >= 2) & (row < 6), jnp.abs(groups[3]) + jnp.abs(groups[7]), 0.0)

    @pl.when(jnp.max(more) > 0.0)
    def _():
        for q in (1, 2):
            for i, value in enumerate(rim(q)):
                rim_ref[i] += value


def final_kernel(
    e_ref, h_ref, s_ref, right_ref, left_ref, up_ref, down_ref, src_ref, rim_ref, fwd_hbm, e_hbm, h_hbm, g_hbm,
    e1_ref, h1_ref, ca_ref, cb_ref, fwd_ref, e_out, h_out, g_out, sems,
):
    nx, ny, nz = s_ref.shape[1], s_ref.shape[2], s_ref.shape[3]
    fetch = pltpu.make_async_copy(fwd_hbm, fwd_ref, sems.at[0])
    fetch.start()
    sub = iota((8, nz), 0)
    ring = iota((ny + 8, nz), 0)

    def tail_of(field, c, x):
        at = x + 2
        ua, ub, da, db = up_ref[at], up_ref[nx + 4 + at], down_ref[at], down_ref[nx + 4 + at]
        if field == 0:
            return jnp.where(sub < 2, turn(da, -2 * c, 0), jnp.where(sub >= 6, turn(ua, 6 - 2 * c, 0), 0.0))
        if field == 1:
            return jnp.where(sub < 1, turn(db, -c, 0), jnp.where(sub >= 6, turn(ub, 6 - 2 * c, 0), 0.0))
        below, above = ((turn(da, 2, 0), turn(ua, 1, 0)), (turn(da, 1, 0), ua), (turn(db, 5, 0), turn(ub, 1, 0)))[c]
        return jnp.where(sub == 0, below, jnp.where(sub == 7, above, 0.0))

    def plane(field, c, x):
        head = plane_of((e_ref, h_ref, s_ref), right_ref, left_ref, field, c, x)
        return None if head is None else jnp.concatenate([head, tail_of(field, c, x)], axis=0)

    def source(c, x):
        tail = jnp.zeros((8, nz), F32)
        if x < 0:
            if c == 0:
                tail = jnp.where(sub == 0, rim_ref[7, 0:1], tail)
            return jnp.concatenate([rim_ref[c], tail], axis=0)
        if x == nx:
            return jnp.concatenate([rim_ref[2], jnp.where(sub == 7, rim_ref[6, 0:1], tail)], axis=0)
        tail = jnp.where(sub == 7, rim_ref[3 + c, x:x + 1], tail)
        if c == 0:
            tail = jnp.where(sub == 0, rim_ref[5, x:x + 1], tail)
        return jnp.concatenate([src_ref[c, x], tail], axis=0)

    before = None
    now = [plane(0, c, -2) for c in range(3)]
    for x in range(-2, nx + 1):
        e, now = now, [plane(0, c, x + 1) for c in range(3)]
        curl = curl_electric(e, now)
        sigma = [plane(2, c, x) for c in range(3)]
        h = []
        for c in range(3):
            value = plane(1, c, x) - 0.5 * curl[c]
            if x > -2:
                outside = sigma[1] <= 0.0
                value = jnp.where(outside if x == -1 else outside & (ring == ny + 7), 0.0, value)
            h.append(value)
            if -1 <= x < nx:
                h1_ref[c, x + 1] = value
        if x > -2:
            drive = curl_magnetic(h, before)
            for c in range(3):
                ca, cb = coefficients(sigma[c])
                inside = sigma[c] > 0.0
                if 0 <= x < nx:
                    ca_ref[c, x] = ca[0:ny]
                cb_ref[c, x + 1] = jnp.where(inside, cb, 0.0)
                if c < 2:
                    if (c, x) != (0, nx):
                        drive_c = drive[c] + source(c, x)
                    else:
                        drive_c = drive[c]
                else:
                    drive_c = drive[c]
                e1_ref[c, x + 1] = jnp.where(inside, ca * e[c] + cb * drive_c, 0.0)
        before = h
    fetch.wait()
    before = None
    sends = []
    for x in range(-1, nx):
        e = [e1_ref[c, x + 1] for c in range(3)]
        curl = curl_electric(e, [e1_ref[c, x + 2] for c in range(3)])
        inside = cb_ref[1, x + 1] > 0.0
        h = [jnp.where(inside, h1_ref[c, x + 1] - 0.5 * curl[c], 0.0) for c in range(3)]
        if x >= 0:
            drive = curl_magnetic(h, before)
            for c in range(3):
                ca, cb = ca_ref[c, x], cb_ref[c, x + 1, 0:ny]
                push = drive[c][0:ny]
                if c < 2:
                    push = push + src_ref[2 + c, x]
                old = e[c][0:ny]
                after = ca * old + cb * push
                h_out[c, x] = h[c][0:ny]
                e_out[c, x] = after
                g_out[c, x] = fwd_ref[0, c, x].astype(F32) * old + fwd_ref[1, c, x].astype(F32) * after
            if x % 4 == 3:
                span = pl.ds(x - 3, 4)
                for near, far in ((e_out, e_hbm), (h_out, h_hbm), (g_out, g_hbm)):
                    sends.append(pltpu.make_async_copy(near.at[:, span], far.at[:, span], sems.at[1 + len(sends)]))
                    sends[-1].start()
        before = h
    for send in sends:
        send.wait()


def body(e_adjoint, h_adjoint, sigma, e_forward, misfit, dest_tile, recv_cell, time_weights):
    tiles = lax.axis_size("gx")
    rows = misfit.shape[0]
    grid = e_adjoint.shape
    nx, ny, nz = grid[1:]
    wide = (ny + 8, nz)
    parts = 3
    lines = misfit.reshape(rows, 2, 2, 128).transpose(0, 2, 1, 3).reshape(rows * 4, 128)
    fields, right, left = call(
        functools.partial(rows_kernel, rows, parts),
        [lines, dest_tile.reshape(1, rows), recv_cell, time_weights, e_adjoint, h_adjoint, sigma],
        [((8, rows), F32), ((3, 5, ny, nz), F32), ((3, 4, ny, nz), F32)],
        scratch=[pltpu.VMEM((rows * 4, 128), F32), pltpu.VMEM((1, rows), jnp.int32), pltpu.VMEM((rows,), jnp.int32),
                 pltpu.VMEM(time_weights.shape, F32), pltpu.SemaphoreType.DMA((parts + 3,)), pltpu.SemaphoreType.DMA((6,))],
        far_in=range(7), name="rows", room=58,
    )
    rows_up, rows_down = shift(fields, "gy", 1), shift(fields, "gy", -1)
    right, left = shift(right, "gx", 1), shift(left, "gx", -1)
    own, = call(functools.partial(own_kernel, tiles), [fields], [((tiles, 8, 128), F32)], flops=4 * 2 * 256 * rows * 128, name="own")
    packed, = call(functools.partial(message_kernel, tiles), [own, rows_up, rows_down], [((tiles, 8, 128), F32)], flops=8 * 2 * 256 * rows * 128, name="message")
    packed, right, left = lax.optimization_barrier((packed, right, left))
    received = lax.all_to_all(packed, "gx", split_axis=0, concat_axis=0, tiled=True)
    side = ((2 * (nx + 4), 8, nz), F32)
    up, down = call(side_kernel, [e_adjoint, h_adjoint, sigma, right, left], [side, side], name="sides")
    up, down = shift(up, "gy", 1), shift(down, "gy", -1)
    source, rim = call(
        functools.partial(scatter_kernel, tiles), [received], [((4,) + grid[1:], F32), ((8, 16, nz), F32)],
        flops=2 * 8 * 256 * 2048 * 256, name="scatter", room=24,
    )
    return call(
        final_kernel, [e_adjoint, h_adjoint, sigma, right, left, up, down, source, rim, e_forward], [(grid, F32)] * 3,
        scratch=[pltpu.VMEM((3, nx + 2) + wide, F32), pltpu.VMEM((3, nx + 1) + wide, F32), pltpu.VMEM(grid, F32), pltpu.VMEM((3, nx + 2) + wide, F32),
                 pltpu.VMEM(e_forward.shape, BF16), pltpu.VMEM(grid, F32), pltpu.VMEM(grid, F32), pltpu.VMEM(grid, F32),
                 pltpu.SemaphoreType.DMA((13,))],
        far_in=(9,), far_out=(0, 1, 2), name="final",
    )


def solution(mesh):
    placed = (
        P(None, "gx", "gy", None),
        P(None, "gx", "gy", None),
        P(None, "gx", "gy", None),
        P(None, None, "gx", "gy", None),
        P(("gx", "gy"), None, None),
        P(("gx", "gy"), None),
        P(("gx", "gy")),
        P(),
    )
    return jax.shard_map(
        body,
        mesh=mesh,
        in_specs=placed,
        out_specs=(P(None, "gx", "gy", None), P(None, "gx", "gy", None), P(None, "gx", "gy", None)),
        check_vma=False,
    )
```

```python
import functools

import jax
import jax.numpy as jnp
from jax import lax
from jax.experimental import pallas as pl
from jax.experimental.pallas import tpu as pltpu
from jax.sharding import PartitionSpec as P

STEPS = 2
CAP = 48
NT = (((1,), (1,)), ((), ()))
VMEM = pl.BlockSpec(memory_space=pltpu.VMEM)
FAR = pl.BlockSpec(memory_space=pltpu.HBM)
F32 = jnp.float32
BF16 = jnp.bfloat16


def shift(block, axis, distance):
    count = lax.axis_size(axis)
    return lax.ppermute(block, axis, [(i, (i + distance) % count) for i in range(count)])


def call(kernel, args, outs, scratch=(), flops=0, name=None, far_in=(), far_out=(), room=16):
    outs = [jax.ShapeDtypeStruct(shape, dtype) for shape, dtype in outs]
    moved = sum(a.size * a.dtype.itemsize for a in list(args) + outs)
    return pl.pallas_call(
        kernel,
        out_shape=outs,
        in_specs=[FAR if i in far_in else VMEM for i in range(len(args))],
        out_specs=[FAR if i in far_out else VMEM for i in range(len(outs))],
        scratch_shapes=list(scratch),
        compiler_params=pltpu.CompilerParams(vmem_limit_bytes=room * 1024 * 1024),
        cost_estimate=pl.CostEstimate(flops=flops, bytes_accessed=moved, transcendentals=0),
        name=name,
    )(*args)


def iota(shape, axis):
    return lax.broadcasted_iota(jnp.int32, shape, axis)


def hot(condition):
    return jnp.where(condition, 1.0, 0.0).astype(BF16)


def pieces(value):
    high = value.astype(BF16)
    return high, (value - high.astype(F32)).astype(BF16)


def turn(a, amount, axis):
    amount = amount % a.shape[axis]
    return a if amount == 0 else pltpu.roll(a, amount, axis)


def z_up(a):
    return jnp.where(iota(a.shape, 1) == a.shape[1] - 1, 0.0, turn(a, -1, 1))


def z_low(a):
    return jnp.where(iota(a.shape, 1) == 0, 0.0, turn(a, 1, 1))


def y_up(a):
    return turn(a, -1, 0)


def y_low(a):
    return turn(a, 1, 0)


def clear_ends(axis, onward_ref, back_ref):
    place = lax.axis_index(axis)

    @pl.when(place == lax.axis_size(axis) - 1)
    def _():
        onward_ref[...] = jnp.zeros(onward_ref.shape, F32)

    @pl.when(place == 0)
    def _():
        back_ref[...] = jnp.zeros(back_ref.shape, F32)


def edge_copies(e_hbm, h_hbm, s_hbm, right_ref, left_ref, sems):
    nx = e_hbm.shape[1]
    plan = (
        (e_hbm, nx - 2, 2, right_ref, 0), (h_hbm, nx - 2, 2, right_ref, 2), (s_hbm, nx - 1, 1, right_ref, 4),
        (e_hbm, 0, 2, left_ref, 0), (h_hbm, 0, 1, left_ref, 2), (s_hbm, 0, 1, left_ref, 3),
    )
    return [
        pltpu.make_async_copy(source.at[:, pl.ds(x, count)], target.at[:, pl.ds(first, count)], sems.at[at])
        for at, (source, x, count, target, first) in enumerate(plan)
    ]


def rows_kernel(
    rows, parts, misfit_hbm, dest_hbm, cell_hbm, weights_hbm, e_hbm, h_hbm, s_hbm, own_ref, right_ref, left_ref,
    misfit_ref, dest_ref, cell_ref, weights_ref, sems, edge_sems,
):
    depth = 4 * rows // parts
    copies = [
        pltpu.make_async_copy(dest_hbm, dest_ref, sems.at[parts]),
        pltpu.make_async_copy(weights_hbm, weights_ref, sems.at[parts + 1]),
        pltpu.make_async_copy(cell_hbm, cell_ref, sems.at[parts + 2]),
    ]
    for part in range(parts):
        span = pl.ds(part * depth, depth)
        copies.append(pltpu.make_async_copy(misfit_hbm.at[span], misfit_ref.at[span], sems.at[part]))
    copies.extend(edge_copies(e_hbm, h_hbm, s_hbm, right_ref, left_ref, edge_sems))
    for copy in copies:
        copy.start()
    for copy in copies[0:3]:
        copy.wait()
    rest = weights_ref[...]
    stack = []
    for _ in range(3):
        stack.append(rest.astype(BF16).astype(F32))
        rest = rest - stack[-1]
    stacked = jnp.concatenate(stack + [jnp.zeros((10, rest.shape[1]), F32)], axis=0).astype(BF16)
    row = iota((8, rows), 0)
    fields = jnp.where(row == 4, cell_ref[...].reshape(1, rows).astype(F32), 0.0)
    fields = jnp.where(row == 5, dest_ref[...].astype(F32), fields)
    own_ref[...] = fields
    for part in range(parts):
        copies[3 + part].wait()
        count = rows // parts
        line = iota((4, count), 0)
        amps = jnp.zeros((4, count), F32)
        for comp in range(2):
            start = part * depth + comp
            block = jnp.concatenate([misfit_ref[pl.ds(start + 2 * half, count, stride=4), :] for half in range(2)], axis=1)
            high, low = [lax.dot_general(stacked, piece, NT, preferred_element_type=F32) for piece in pieces(block)]
            for k in range(STEPS):
                amp = high[k:k + 1] + (high[2 + k:3 + k] + low[k:k + 1]) + (high[4 + k:5 + k] + low[2 + k:3 + k])
                amps = jnp.where(line == 2 * k + comp, amp, amps)
        own_ref[0:4, part * count:(part + 1) * count] = amps
    for copy in copies[3 + parts:]:
        copy.wait()
    clear_ends("gx", right_ref, left_ref)


def plane_of(refs, right_ref, left_ref, field, c, x):
    nx = refs[0].shape[1]
    if 0 <= x < nx:
        return refs[field][c, x]
    at = {(0, -2): 0, (0, -1): 1, (1, -2): 2, (1, -1): 3, (2, -1): 4}.get((field, x))
    if at is not None:
        return right_ref[c, at]
    at = {(0, nx): 0, (0, nx + 1): 1, (1, nx): 2, (2, nx): 3}.get((field, x))
    return None if at is None else left_ref[c, at]


def side_kernel(e_ref, h_ref, s_ref, right_ref, left_ref, up_ref, down_ref):
    nx, nz = e_ref.shape[1], e_ref.shape[3]
    sub = iota((8, nz), 0)
    zero = jnp.zeros((16, nz), F32)
    for x in range(-2, nx + 2):
        planes = [[plane_of((e_ref, h_ref, s_ref), right_ref, left_ref, f, c, x) for c in range(3)] for f in range(3)]
        planes = [[zero if p is None else p for p in group] for group in planes]
        e, h, s = [[p[8:16] for p in group] for group in planes]
        three = [jnp.where(sub < 2, turn(f[0], 2, 0), jnp.where(sub < 4, turn(f[1], 4, 0), turn(f[2], 6, 0))) for f in (e, h)]
        at, other = x + 2, nx + 6 + x
        up_ref[at] = jnp.where(sub < 6, three[0], jnp.where(sub == 6, turn(s[0], 7, 0), s[1]))
        up_ref[other] = jnp.where(sub < 6, three[1], jnp.where(sub == 6, turn(s[2], 7, 0), 0.0))
        e, h, s = [[p[0:8] for p in group] for group in planes]
        three = jnp.where(sub < 2, e[0], jnp.where(sub < 4, turn(e[1], 2, 0), turn(e[2], 4, 0)))
        down_ref[at] = jnp.where(sub < 6, three, jnp.where(sub == 6, turn(s[0], 6, 0), turn(s[1], 7, 0)))
        three = jnp.where(sub == 0, h[0], jnp.where(sub == 1, turn(h[1], 1, 0), turn(h[2], 2, 0)))
        down_ref[other] = jnp.where(sub < 3, three, jnp.where(sub == 3, turn(s[2], 3, 0), 0.0))
    clear_ends("gy", up_ref, down_ref)


def parse(fields):
    dest = fields[5:6].astype(jnp.int32)
    cell = fields[4:5].astype(jnp.int32)
    return dest, cell // 4096, (cell // 256) % 16


def ranks(groups, tiles):
    rows = groups[0].shape[1]
    named = [(iota((tiles, rows), 0) == group).astype(F32) for group in groups]
    earlier = hot(iota((rows, rows), 0) < iota((rows, rows), 1))
    before = jnp.dot(jnp.concatenate(named, axis=0).astype(BF16), earlier, preferred_element_type=F32)
    return [
        jnp.sum(one * before[tiles * n:tiles * (n + 1)], axis=0, keepdims=True).astype(jnp.int32) for n, one in enumerate(named)
    ]


def lay(fields, lane, picks):
    tiles, rows = 32, fields.shape[1]
    row = iota((8, rows), 0)
    left = [jnp.zeros((8, rows), BF16).astype(F32)] * 2
    where = jnp.full((8, rows), -1, jnp.int32)
    for at, field, tile in picks:
        for number, part in enumerate(pieces(fields[field:field + 1])):
            left[number] = jnp.where(row == at, part.astype(F32), left[number])
        where = jnp.where(row == at, tile, where)
    mask = iota((tiles, 8, rows), 0) == where[None]
    spread = hot(iota((128, rows), 0) == lane)
    total = None
    for part in left:
        block = jnp.where(mask, part[None], 0.0).reshape(tiles * 8, rows).astype(BF16)
        product = lax.dot_general(block, spread, NT, preferred_element_type=F32)
        total = product if total is None else total + product
    return total.reshape(tiles, 8, 128)


def corner_picks(rank, field, tile):
    picks = []
    for group in range(3):
        here = jnp.where(rank // 16 == group, tile, -1)
        picks += [(2 * group, field, here), (2 * group + 1, 4, here)]
    return picks


def own_kernel(tiles, fields_ref, out_ref):
    fields = fields_ref[...]
    dest, x, _ = parse(fields)
    after = jnp.where(x == 15, dest + 1, -1)
    ahead = jnp.where(x == 0, dest - 1, -1)
    slot, rank_after, rank_ahead = ranks([dest, after, ahead], tiles)
    block = lay(fields, slot, [(i, i, dest) for i in range(5)])
    block = block + lay(fields, rank_after + 64, [(0, 0, after), (1, 1, after), (2, 4, after)])
    out_ref[...] = block + lay(fields, rank_ahead + 64, [(3, 1, ahead), (4, 4, ahead)])


def message_kernel(tiles, own_ref, up_ref, down_ref, out_ref):
    place = lax.axis_index("gy")
    fields = jnp.where(place > 0, up_ref[...], 0.0)
    dest, x, y = parse(fields)
    here = jnp.where(y == 15, dest, -1)
    ahead = jnp.where((y == 15) & (x == 0), dest - 1, -1)
    rank, corner = ranks([here, ahead], tiles)
    block = own_ref[...] + lay(fields, rank, [(5, 0, here), (6, 1, here), (7, 4, here)])
    block = block + lay(fields, 48 + corner % 16, corner_picks(corner, 1, ahead))
    fields = jnp.where(place < lax.axis_size("gy") - 1, down_ref[...], 0.0)
    dest, x, y = parse(fields)
    filled = (fields[0:1] != 0.0) | (fields[1:2] != 0.0) | (fields[2:3] != 0.0) | (fields[3:4] != 0.0)
    here = jnp.where((y == 0) & filled, dest, -1)
    after = jnp.where((y == 0) & (x == 15) & filled, dest + 1, -1)
    rank, corner = ranks([here, after], tiles)
    block = block + lay(fields, rank + 64, [(5, 0, here), (6, 4, here)])
    out_ref[...] = block + lay(fields, 112 + corner % 16, corner_picks(corner, 0, after))


def coefficients(sigma):
    half = 0.5 * sigma
    under = 1.0 / (1.0 + half)
    return (1.0 - half) * under, 0.5 * under


def curl_electric(e, after):
    ex, ey, ez = e
    cx = (y_up(ez) - ez) - (z_up(ey) - ey)
    cy = (z_up(ex) - ex) - (after[2] - ez)
    cz = (after[1] - ey) - (y_up(ex) - ex)
    return cx, cy, cz


def curl_magnetic(h, before):
    hx, hy, hz = h
    cx = (hz - y_low(hz)) - (hy - z_low(hy))
    cy = (hx - z_low(hx)) - (hz - before[2])
    cz = (hy - before[1]) - (hx - y_low(hx))
    return cx, cy, cz


def listed(table, amps, cell_row, position, count, nz):
    cell = table[cell_row:cell_row + 1].astype(jnp.int32)
    depth_hot = hot(iota((nz, table.shape[1]), 0) == cell % nz)
    held = hot(iota((count, table.shape[1]), 0) == position(cell // nz))
    left = jnp.concatenate([held * part[a:a + 1] for a in amps for part in pieces(table)], axis=0)
    product = lax.dot_general(left, depth_hot, NT, preferred_element_type=F32)
    return [
        product[2 * i * count:(2 * i + 1) * count] + product[(2 * i + 1) * count:(2 * i + 2) * count] for i in range(len(amps))
    ]


def scatter_kernel(tiles, recv_ref, src_ref, rim_ref):
    nx, ny, nz = src_ref.shape[1:]
    lane = iota((8, 128), 1)
    row = iota((8, tiles * 16), 0)

    def group(number):
        out = []
        for first in range(0, tiles, 8):
            merged = None
            for at in range(8):
                moved = turn(recv_ref[first + at], 16 * (at - number), 1)
                merged = moved if merged is None else jnp.where(lane // 16 == at, moved, merged)
            out.append(merged)
        return jnp.concatenate(out, axis=1)

    groups = [group(number) for number in range(8)]
    table = jnp.concatenate(groups[0:3], axis=1)
    depth = table.shape[1]
    cell = table[4:5].astype(jnp.int32)
    column_hot = hot(iota((nx * ny, depth), 0) == cell // nz)
    depth_hot = hot(iota((nz, depth), 0) == cell % nz)
    parts = pieces(table)
    for i in range(4):
        product = None
        for part in parts:
            term = lax.dot_general(column_hot * part[i:i + 1], depth_hot, NT, preferred_element_type=F32)
            product = term if product is None else product + term
        src_ref[i] = product.reshape(nx, ny, nz)

    def rim(q):
        sums = listed(groups[4 + q], (0, 1), 2, lambda column: column % ny, ny, nz)
        sums += listed(groups[4 + q], (3,), 4, lambda column: column % ny, ny, nz)
        sums += listed(groups[q], (5, 6), 7, lambda column: column // ny, nx, nz)
        sums += listed(groups[4 + q], (5,), 6, lambda column: column // ny, nx, nz)
        sums += listed(groups[3], (2 * q,), 2 * q + 1, lambda column: column * 0, 16, nz)
        return sums + listed(groups[7], (2 * q,), 2 * q + 1, lambda column: column * 0, 16, nz)

    for i, value in enumerate(rim(0)):
        rim_ref[i] = value
    more = jnp.where(row >= 5, jnp.abs(groups[1]) + jnp.abs(groups[2]), 0.0)
    more = more + jnp.where(row < 7, jnp.abs(groups[5]) + jnp.abs(groups[6]), 0.0)
    more = more + jnp.where((row >= 2) & (row < 6), jnp.abs(groups[3]) + jnp.abs(groups[7]), 0.0)

    @pl.when(jnp.max(more) > 0.0)
    def _():
        for q in (1, 2):
            for i, value in enumerate(rim(q)):
                rim_ref[i] += value


def first_kernel(e_ref, h_ref, s_ref, right_ref, left_ref, up_ref, down_ref, e1_ref, h1_ref, cb_ref):
    nx, ny, nz = s_ref.shape[1], s_ref.shape[2], s_ref.shape[3]
    sub = iota((8, nz), 0)
    ring = iota((ny + 8, nz), 0)

    def tail_of(field, c, x):
        at = x + 2
        ua, ub, da, db = up_ref[at], up_ref[nx + 4 + at], down_ref[at], down_ref[nx + 4 + at]
        if field == 0:
            return jnp.where(sub < 2, turn(da, -2 * c, 0), jnp.where(sub >= 6, turn(ua, 6 - 2 * c, 0), 0.0))
        if field == 1:
            return jnp.where(sub < 1, turn(db, -c, 0), jnp.where(sub >= 6, turn(ub, 6 - 2 * c, 0), 0.0))
        below, above = ((turn(da, 2, 0), turn(ua, 1, 0)), (turn(da, 1, 0), ua), (turn(db, 5, 0), turn(ub, 1, 0)))[c]
        return jnp.where(sub == 0, below, jnp.where(sub == 7, above, 0.0))

    def plane(field, c, x):
        head = plane_of((e_ref, h_ref, s_ref), right_ref, left_ref, field, c, x)
        return None if head is None else jnp.concatenate([head, tail_of(field, c, x)], axis=0)

    before = None
    now = [plane(0, c, -2) for c in range(3)]
    for x in range(-2, nx + 1):
        e, now = now, [plane(0, c, x + 1) for c in range(3)]
        curl = curl_electric(e, now)
        sigma = [plane(2, c, x) for c in range(3)]
        h = []
        for c in range(3):
            value = plane(1, c, x) - 0.5 * curl[c]
            if x > -2:
                outside = sigma[1] <= 0.0
                value = jnp.where(outside if x == -1 else outside & (ring == ny + 7), 0.0, value)
            h.append(value)
            if -1 <= x < nx:
                h1_ref[c, x + 1] = value
        if x > -2:
            drive = curl_magnetic(h, before)
            for c in range(3):
                ca, cb = coefficients(sigma[c])
                inside = sigma[c] > 0.0
                if c < 2:
                    cb_ref[c, x + 1] = jnp.where(inside, cb, 0.0)
                e1_ref[c, x + 1] = jnp.where(inside, ca * e[c] + cb * drive[c], 0.0)
        before = h


def last_kernel(
    s_ref, e0_ref, h1_ref, cb_ref, src_ref, rim_ref, fwd_hbm, e_hbm, h_hbm, g_hbm,
    fwd_ref, e_out, h_out, g_out, sems,
):
    nx, ny, nz = s_ref.shape[1], s_ref.shape[2], s_ref.shape[3]
    fetch = pltpu.make_async_copy(fwd_hbm, fwd_ref, sems.at[0])
    fetch.start()
    sub = iota((8, nz), 0)

    def source(c, x):
        tail = jnp.zeros((8, nz), F32)
        if x < 0:
            if c == 0:
                tail = jnp.where(sub == 0, rim_ref[7, 0:1], tail)
            return jnp.concatenate([rim_ref[c], tail], axis=0)
        if x == nx:
            return jnp.concatenate([rim_ref[2], jnp.where(sub == 7, rim_ref[6, 0:1], tail)], axis=0)
        tail = jnp.where(sub == 7, rim_ref[3 + c, x:x + 1], tail)
        if c == 0:
            tail = jnp.where(sub == 0, rim_ref[5, x:x + 1], tail)
        return jnp.concatenate([src_ref[c, x], tail], axis=0)

    def electric(c, x):
        old = e0_ref[c, x + 1]
        if c == 2 or (c, x) == (0, nx):
            return old
        return old + cb_ref[c, x + 1] * source(c, x)

    fetch.wait()
    before = None
    sends = []
    now = [electric(c, -1) for c in range(3)]
    for x in range(-1, nx):
        e, now = now, [electric(c, x + 1) for c in range(3)]
        curl = curl_electric(e, now)
        inside = cb_ref[1, x + 1] > 0.0
        h = [jnp.where(inside, h1_ref[c, x + 1] - 0.5 * curl[c], 0.0) for c in range(3)]
        if x >= 0:
            drive = curl_magnetic(h, before)
            for c in range(3):
                ca, cb = coefficients(s_ref[c, x])
                push = drive[c][0:ny]
                if c < 2:
                    push = push + src_ref[2 + c, x]
                old = e[c][0:ny]
                after = ca * old + cb * push
                h_out[c, x] = h[c][0:ny]
                e_out[c, x] = after
                g_out[c, x] = fwd_ref[0, c, x].astype(F32) * old + fwd_ref[1, c, x].astype(F32) * after
            if x % 4 == 3:
                span = pl.ds(x - 3, 4)
                for near, far in ((e_out, e_hbm), (h_out, h_hbm), (g_out, g_hbm)):
                    sends.append(pltpu.make_async_copy(near.at[:, span], far.at[:, span], sems.at[1 + len(sends)]))
                    sends[-1].start()
        before = h
    for send in sends:
        send.wait()


def body(e_adjoint, h_adjoint, sigma, e_forward, misfit, dest_tile, recv_cell, time_weights):
    tiles = lax.axis_size("gx")
    rows = misfit.shape[0]
    grid = e_adjoint.shape
    nx, ny, nz = grid[1:]
    wide = (ny + 8, nz)
    parts = 3
    lines = misfit.reshape(rows, 2, 2, 128).transpose(0, 2, 1, 3).reshape(rows * 4, 128)
    fields, right, left = call(
        functools.partial(rows_kernel, rows, parts),
        [lines, dest_tile.reshape(1, rows), recv_cell, time_weights, e_adjoint, h_adjoint, sigma],
        [((8, rows), F32), ((3, 5, ny, nz), F32), ((3, 4, ny, nz), F32)],
        scratch=[pltpu.VMEM((rows * 4, 128), F32), pltpu.VMEM((1, rows), jnp.int32), pltpu.VMEM((rows,), jnp.int32),
                 pltpu.VMEM(time_weights.shape, F32), pltpu.SemaphoreType.DMA((parts + 3,)), pltpu.SemaphoreType.DMA((6,))],
        far_in=range(7), name="rows", room=58,
    )
    rows_up, rows_down = shift(fields, "gy", 1), shift(fields, "gy", -1)
    right, left = shift(right, "gx", 1), shift(left, "gx", -1)
    own, = call(functools.partial(own_kernel, tiles), [fields], [((tiles, 8, 128), F32)], flops=4 * 2 * 256 * rows * 128, name="own")
    packed, = call(functools.partial(message_kernel, tiles), [own, rows_up, rows_down], [((tiles, 8, 128), F32)], flops=8 * 2 * 256 * rows * 128, name="message")
    packed, right, left = lax.optimization_barrier((packed, right, left))
    received = lax.all_to_all(packed, "gx", split_axis=0, concat_axis=0, tiled=True)
    side = ((2 * (nx + 4), 8, nz), F32)
    up, down = call(side_kernel, [e_adjoint, h_adjoint, sigma, right, left], [side, side], name="sides")
    up, down = shift(up, "gy", 1), shift(down, "gy", -1)
    e1, h1, cb = call(
        first_kernel, [e_adjoint, h_adjoint, sigma, right, left, up, down],
        [((3, nx + 2) + wide, F32), ((3, nx + 1) + wide, F32), ((2, nx + 2) + wide, F32)], name="first",
    )
    received, e1, h1, cb = lax.optimization_barrier((received, e1, h1, cb))
    source, rim = call(
        functools.partial(scatter_kernel, tiles), [received], [((4,) + grid[1:], F32), ((8, 16, nz), F32)],
        flops=2 * 8 * 256 * 2048 * 256, name="scatter", room=24,
    )
    return call(
        last_kernel, [sigma, e1, h1, cb, source, rim, e_forward], [(grid, F32)] * 3,
        scratch=[pltpu.VMEM(e_forward.shape, BF16), pltpu.VMEM(grid, F32), pltpu.VMEM(grid, F32), pltpu.VMEM(grid, F32),
                 pltpu.SemaphoreType.DMA((13,))],
        far_in=(6,), far_out=(0, 1, 2), name="last",
    )


def solution(mesh):
    placed = (
        P(None, "gx", "gy", None),
        P(None, "gx", "gy", None),
        P(None, "gx", "gy", None),
        P(None, None, "gx", "gy", None),
        P(("gx", "gy"), None, None),
        P(("gx", "gy"), None),
        P(("gx", "gy")),
        P(),
    )
    return jax.shard_map(
        body,
        mesh=mesh,
        in_specs=placed,
        out_specs=(P(None, "gx", "gy", None), P(None, "gx", "gy", None), P(None, "gx", "gy", None)),
        check_vma=False,
    )
```
